32 devices in a mesh: section: 2 (over x), dp: 16 (over z, y, core).
Axes of the slice: x: 2, y: 2, z: 4, core: 2. Of those that a mesh axis runs over, the one named last changes fastest.
Arguments:
- x_input: bfloat16 [16384, 768], P('dp'), may hold values from -6 to 6
- w_qkv: bfloat16 [2, 768, 2304], P('section'), may hold values from -0.21875 to 0.21875
- bias_query: float32 [2, 768], P('section'), may hold values from -4 to 4
- bias_value: float32 [2, 768], P('section'), may hold values from -1.5 to 1.5
- w_out: bfloat16 [2, 768, 768], P('section'), may hold values from -0.875 to 0.875
- bias_out: float32 [2, 768], P('section'), may hold values from -1.5 to 1.5
- gain_attn: float32 [2, 768], P('section'), may hold values from 0.5 to 1.5
- shift_attn: float32 [2, 768], P('section'), may hold values from -3 to 3
- w_in: bfloat16 [2, 768, 3072], P('section'), may hold values from -0.21875 to 0.21875
- bias_in: float32 [2, 3072], P('section'), may hold values from -1.5 to 1.5
- w_back: bfloat16 [2, 3072, 768], P('section'), may hold values from -0.109375 to 0.109375
- bias_back: float32 [2, 768], P('section'), may hold values from -1.5 to 1.5
- gain_ffn: float32 [2, 768], P('section'), may hold values from 0.5 to 1.5
- shift_ffn: float32 [2, 768], P('section'), may hold values from -3 to 3
- lengths: int32 [32], P('dp'), may hold values from 160 to 512, as said below
- cotangent: bfloat16 [16384, 768], P('dp'), may hold values from -6 to 6
Outputs:
- activations: bfloat16 [2, 16384, 768], P('section', 'dp')
- input_grads: float32 [2, 16384, 768], P('section', 'dp')
- grad_w_qkv: float32 [2, 768, 2304], P('section')
- grad_bias_query: float32 [2, 768], P('section')
- grad_bias_value: float32 [2, 768], P('section')
- grad_w_out: float32 [2, 768, 768], P('section')
- grad_bias_out: float32 [2, 768], P('section')
- grad_gain_attn: float32 [2, 768], P('section')
- grad_shift_attn: float32 [2, 768], P('section')
- grad_w_in: float32 [2, 768, 3072], P('section')
- grad_bias_in: float32 [2, 3072], P('section')
- grad_w_back: float32 [2, 3072, 768], P('section')
- grad_bias_back: float32 [2, 768], P('section')
- grad_gain_ffn: float32 [2, 768], P('section')
- grad_shift_ffn: float32 [2, 768], P('section')
The draws below stay inside these ranges and needn't reach their ends.
Inputs may be any that keep to these rules, and one draw needn't show every extreme that they name: Passage lengths in tokens; some passage is exactly 512 long.
All inputs are finite; a program needn't handle non-finite values.
Results may differ from the reference program's by a relative error of at most 0.022.
Values may be sent and summed in bfloat16 or wider, within the bound.
A program may use at most 320 MiB of HBM per device.

```python
import math
import jax
import jax.numpy as jnp
from jax import lax

D = 768
HEADS = 12
HEAD = 64
FF = 3072
LEN = 512
MB = 2
PAS = 1
PASSAGES = 32
ROWS = 16384
N_DP = 16


def draw_lengths(key, part):
    key = jax.random.fold_in(key, 7)
    keys = jax.random.split(key, 3)
    shortest = LEN * 5 // 16
    spread = LEN - shortest + 1
    first = jax.random.randint(keys[0], (PASSAGES,), 0, spread)
    second = jax.random.randint(keys[1], (PASSAGES,), 0, spread)
    drawn = shortest + jnp.minimum(first, second)
    chosen = jax.random.randint(keys[2], (), 0, PASSAGES)
    return jnp.where(jnp.arange(PASSAGES) == chosen, LEN, drawn).astype(jnp.int32)


def levels(stream_key, dims, pieces, low, high):
    loudness = 1.0
    for axis_at, shards_of in pieces:
        draws = jax.random.uniform(jax.random.fold_in(jax.random.fold_in(stream_key, 6), axis_at), (shards_of,), jnp.float32, low / len(pieces), high / len(pieces))
        loudness = loudness * jnp.repeat(jnp.exp(draws), dims[axis_at] // shards_of).reshape((-1,) + (1,) * (len(dims) - 1 - axis_at))
    return loudness


def noise(stream_key, dims, scale, limit, pieces=(), kind=jnp.bfloat16):
    gain = levels(stream_key, dims, pieces, -0.22, 0.18) if pieces else 1.0
    values = jax.random.normal(stream_key, dims, jnp.float32) * scale * gain
    return jnp.minimum(jnp.maximum(values, -limit), limit).astype(kind)


def setup_inputs(seed: int = 0) -> dict:
    streams_of = jax.random.split(jax.random.key(seed), 17)
    x_input = noise(streams_of[0], (ROWS, D), 1.0, 6.0, ((0, 16),))
    w_qkv = noise(streams_of[1], (2, D, 3 * D), D ** -0.5, 0.21875, ((0, 2),))
    bias_query = noise(streams_of[2], (2, D), 0.3, 4.0, ((0, 2),), jnp.float32)
    bias_value = noise(streams_of[3], (2, D), 0.1, 1.5, ((0, 2),), jnp.float32)
    w_out = noise(streams_of[4], (2, D, D), (D // 16) ** -0.5, 0.875, ((0, 2),))
    bias_out = noise(streams_of[5], (2, D), 0.1, 1.5, ((0, 2),), jnp.float32)
    gain_attn = jnp.clip(1.0 + 0.1 * jax.random.normal(streams_of[6], (2, D), jnp.float32), 0.5, 1.5)
    shift_attn = noise(streams_of[7], (2, D), 0.2, 3.0, ((0, 2),), jnp.float32)
    w_in = noise(streams_of[8], (2, D, FF), D ** -0.5, 0.21875, ((0, 2),))
    bias_in = noise(streams_of[9], (2, FF), 0.1, 1.5, ((0, 2),), jnp.float32)
    w_back = noise(streams_of[10], (2, FF, D), FF ** -0.5, 0.109375, ((0, 2),))
    bias_back = noise(streams_of[11], (2, D), 0.1, 1.5, ((0, 2),), jnp.float32)
    gain_ffn = jnp.clip(1.0 + 0.1 * jax.random.normal(streams_of[12], (2, D), jnp.float32), 0.5, 1.5)
    shift_ffn = noise(streams_of[13], (2, D), 0.2, 3.0, ((0, 2),), jnp.float32)
    lengths = draw_lengths(jax.random.fold_in(streams_of[16], 71), 0)
    cotangent = noise(streams_of[15], (ROWS, D), 1.0, 6.0, ((0, 16),))
    return dict(x_input=x_input, w_qkv=w_qkv, bias_query=bias_query, bias_value=bias_value, w_out=w_out, bias_out=bias_out, gain_attn=gain_attn, shift_attn=shift_attn, w_in=w_in, bias_in=bias_in, w_back=w_back, bias_back=bias_back, gain_ffn=gain_ffn, shift_ffn=shift_ffn, lengths=lengths, cotangent=cotangent)


@jax.custom_vjp
def low(v):
    return lax.optimization_barrier(v.astype(jnp.bfloat16)).astype(jnp.float32)

@jax.custom_vjp
def low_back(v):
    return v

def low_keep(v):
    return (low(v), None)

def low_pass(kept, grad):
    return (grad,)

def back_keep(v):
    return (v, None)

def back_low(kept, grad):
    return (low(grad),)
low.defvjp(low_keep, low_pass)
low_back.defvjp(back_keep, back_low)

def layer_norm(summed):
    centred = summed - lax.optimization_barrier(jnp.mean(summed, axis=-1, keepdims=True))
    return centred * lax.rsqrt(lax.optimization_barrier(jnp.mean(centred * centred, axis=-1, keepdims=True)) + 1e-12)

def product(left, right):
    return jnp.einsum('gnd,de->gne', left, right, precision=lax.Precision.HIGHEST)

def layer(layer_in, params, live):
    w_qkv, bias_query, bias_value, w_out, bias_out, gain_attn, shift_attn, w_in, bias_in, w_back, bias_back, gain_ffn, shift_ffn = params
    groups, length, model_width = layer_in.shape
    split = (groups, length, HEADS, HEAD)
    projected = product(layer_in, w_qkv)
    queries = low_back(low(projected[..., :model_width] + bias_query)).reshape(split)
    key_part = low_back(low(projected[..., model_width:2 * model_width])).reshape(split)
    value_part = low_back(low(projected[..., 2 * model_width:] + bias_value)).reshape(split)
    scores = jnp.einsum('gqhd,gkhd->ghqk', queries, key_part, precision=lax.Precision.HIGHEST) * (1.0 / math.sqrt(HEAD))
    scores = low_back(scores)
    scores = jnp.where(live[:, None, None, :], scores, -1e+30)
    probs = low(jax.nn.softmax(scores, axis=-1))
    mixed = jnp.einsum('ghqk,gkhd->gqhd', probs, value_part, precision=lax.Precision.HIGHEST)
    mixed = low_back(low(mixed.reshape(groups, length, model_width)))
    attended = low_back(product(mixed, w_out) + bias_out)
    normed = low(layer_norm(layer_in + attended) * gain_attn + shift_attn)
    inner = low_back(product(normed, w_in) + bias_in)
    active = low(jax.nn.gelu(inner, approximate=False))
    outer = low_back(product(active, w_back) + bias_back)
    return layer_norm(normed + outer) * gain_ffn + shift_ffn

def reference(x_input, w_qkv, bias_query, bias_value, w_out, bias_out, gain_attn, shift_attn, w_in, bias_in, w_back, bias_back, gain_ffn, shift_ffn, lengths, cotangent):
    weights = (w_qkv, bias_query, bias_value, w_out, bias_out, gain_attn, shift_attn, w_in, bias_in, w_back, bias_back, gain_ffn, shift_ffn)
    first = tuple((tensor[0].astype(jnp.float32) for tensor in weights))
    second = tuple((tensor[1].astype(jnp.float32) for tensor in weights))
    passages = N_DP * MB * PAS
    group_size = math.gcd(passages, max(1, 4096 // LEN))
    group_count = passages // group_size
    model_width = x_input.shape[1]
    inputs = x_input.astype(jnp.float32).reshape(group_count, group_size, LEN, model_width)
    cots = cotangent.astype(jnp.float32).reshape(group_count, group_size, LEN, model_width)
    spans = lengths.astype(jnp.int32).reshape(group_count, group_size)

    def visit(totals, element):
        block_x, block_cot, block_len = element
        live = jnp.arange(LEN, dtype=jnp.int32)[None, :] < block_len[:, None]

        def sections(layer_in, probe, params_first, params_second):
            sent = low(layer(layer_in, params_first, live))
            top_out = layer(low_back(sent + probe), params_second, live)
            return (top_out, sent)
        top_out, pull, sent = jax.vjp(sections, block_x, jnp.zeros_like(block_x), first, second, has_aux=True)
        grad_x, grad_probe, grad_first, grad_second = pull(block_cot)
        totals = jax.tree.map(jnp.add, totals, (grad_first, grad_second))
        return (totals, (sent.astype(jnp.bfloat16), top_out.astype(jnp.bfloat16), grad_x, grad_probe))
    zero = jax.tree.map(jnp.zeros_like, (first, second))
    totals, outputs = lax.scan(visit, zero, (inputs, cots, spans))
    sent_all, top_all, grad_x, grad_probe = outputs
    shape2 = (N_DP * MB * PAS * LEN, model_width)
    activations = jnp.stack([sent_all.reshape(shape2), top_all.reshape(shape2)])
    input_grads = jnp.stack([grad_x.reshape(shape2), grad_probe.reshape(shape2)])
    grads = tuple((jnp.stack([left, right]) for left, right in zip(totals[0], totals[1])))
    return (activations, input_grads, grads[0], grads[1], grads[2], grads[3], grads[4], grads[5], grads[6], grads[7], grads[8], grads[9], grads[10], grads[11], grads[12])
```

```python
import functools

import jax
import jax.numpy as jnp
from jax import lax
from jax.experimental import pallas as pl
from jax.experimental.pallas import tpu as pltpu
from jax.sharding import PartitionSpec as P

HEAD = 64
LANES = 128
MB = 2
EPSILON = 1e-12
DEAD = -1e30
FACTOR_ATTN = 12
FACTOR_FFN = 13
STAT_COLUMNS = 16
VMEM_LIMIT = 63 << 20

FORWARD_VECTORS = (
    "bias_query",
    "bias_value",
    "bias_out",
    "gain_attn",
    "shift_attn",
    "bias_in",
    "bias_back",
    "gain_ffn",
    "shift_ffn",
)
SUM_ROWS = tuple(name for name in FORWARD_VECTORS if name != "bias_in")
SUM_COUNT = 16

f32 = jnp.float32
bf16 = jnp.bfloat16
MESH = pl.DeviceIdType.MESH
NN = (((1,), (0,)), ((), ()))
NT = (((1,), (1,)), ((), ()))
TN = (((0,), (0,)), ((), ()))


def mm(left, right, dims=NN):
    return lax.dot_general(left, right, dims, preferred_element_type=f32)


def rows_at(index, count):
    return pl.ds(pl.multiple_of(index * count, count), count)


def norm_rows(value):
    centred = value - jnp.mean(value, axis=-1, keepdims=True)
    factor = lax.rsqrt(jnp.mean(centred * centred, axis=-1, keepdims=True) + EPSILON)
    return centred * factor, factor


def norm_back(grad_hat, unit, factor):
    return factor * (
        grad_hat
        - jnp.mean(grad_hat, axis=-1, keepdims=True)
        - unit * jnp.mean(grad_hat * unit, axis=-1, keepdims=True)
    )


def column_sum(value):
    return jnp.sum(value, axis=0, keepdims=True)


def split_three(value):
    high = value.astype(bf16)
    rest = value - high.astype(f32)
    middle = rest.astype(bf16)
    low = (rest - middle.astype(f32)).astype(bf16)
    return high, middle, low


def key_bias(rows, length):
    key = lax.broadcasted_iota(jnp.int32, (rows, LANES), 0)
    return jnp.where(key < length, 0.0, DEAD).astype(bf16)


def attention_forward(qkv, mixed, stats, length, width):
    rows = qkv.shape[0]
    lane = lax.broadcasted_iota(jnp.int32, (rows, LANES), 1)
    dead = key_bias(rows, length)
    zero = jnp.zeros((rows, LANES), bf16)
    one = jnp.ones((rows, LANES), bf16)
    log_totals = []
    for h in range(width // LANES):
        q2, k2, v2 = [qkv[:, pl.ds(part * width + h * LANES, LANES)] for part in range(3)]
        outs = []
        for half in (0, 1):
            own = (lane < HEAD) if half == 0 else (lane >= HEAD)
            at = HEAD if half == 0 else 0
            mark = lane == at
            qa = jnp.where(own, q2, jnp.where(mark, one, zero))
            ka = jnp.where(own, k2, jnp.where(mark, dead, zero))
            va = jnp.where(own, v2, jnp.where(mark, one, zero)).T
            scores = mm(ka, qa, NT)
            highest = jnp.max(scores, axis=0, keepdims=True)
            product = mm(va, jnp.exp(scores - highest).astype(bf16))
            total = product[at : at + 1]
            outs.append(product[HEAD * half : HEAD * half + HEAD] * (1.0 / total))
            log_totals.append(highest + jnp.log(total))
        mixed[:, pl.ds(h * LANES, LANES)] = jnp.concatenate(outs, 0).T.astype(bf16)
    spare = STAT_COLUMNS - len(log_totals)
    log_totals = jnp.concatenate(log_totals + [jnp.zeros((spare, rows), f32)], 0)
    stats[:, :STAT_COLUMNS] = log_totals.T


def forward_block(x, weights, vec, need, length, saved, result, send, done):
    w_qkv, w_out, w_in, w_back = weights
    qkv, mixed, stats, unit1, normed, active, slope, unit2 = saved
    rows, width = x.shape
    half_rows = rows // 2
    need(0)
    scale = HEAD ** -0.5
    qkv[:, :width] = ((mm(x[...], w_qkv[:, :width]) + vec["bias_query"][...]) * scale).astype(bf16)
    qkv[:, width : 2 * width] = mm(x[...], w_qkv[:, width : 2 * width]).astype(bf16)
    qkv[:, 2 * width :] = (mm(x[...], w_qkv[:, 2 * width :]) + vec["bias_value"][...]).astype(bf16)
    done(0)
    attention_forward(qkv, mixed, stats, length, width)
    done(1)
    lane = lax.broadcasted_iota(jnp.int32, (half_rows, LANES), 1)
    need(1)

    def after_attention(block, carry):
        rs = rows_at(block, half_rows)
        summed = x[rs, :].astype(f32) + mm(mixed[rs, :], w_out[...]) + vec["bias_out"][...]
        unit, factor = norm_rows(summed)
        unit1[rs, :] = unit
        normed[rs, :] = (unit * vec["gain_attn"][...] + vec["shift_attn"][...]).astype(bf16)
        stats[rs, :] = jnp.where(lane == FACTOR_ATTN, factor, stats[rs, :])
        return carry

    lax.fori_loop(0, 2, after_attention, 0)
    done(3)
    done(4)
    need(2)

    def hidden(j, carry):
        cs = rows_at(j, width)
        inner = mm(normed[...], w_in[:, cs]) + vec["bias_in"][:, cs]
        share = 0.5 * (1.0 + lax.erf(inner * 0.7071067811865476))
        active[:, cs] = (inner * share).astype(bf16)
        slope[:, cs] = (
            share + inner * jnp.exp(-0.5 * inner * inner) * 0.3989422804014327
        ).astype(bf16)
        return carry

    lax.fori_loop(0, w_in.shape[1] // width, hidden, 0)
    done(5)
    done(6)
    need(3)

    def after_ffn(block, carry):
        rs = rows_at(block, half_rows)
        summed = normed[rs, :].astype(f32) + mm(active[rs, :], w_back[...]) + vec["bias_back"][...]
        unit, factor = norm_rows(summed)
        unit2[rs, :] = unit
        result[rs, :] = (unit * vec["gain_ffn"][...] + vec["shift_ffn"][...]).astype(bf16)
        stats[rs, :] = jnp.where(lane == FACTOR_FFN, factor, stats[rs, :])
        send(block)
        return carry

    lax.fori_loop(0, 2, after_ffn, 0)
    done(2)
    done(7)
    done(9)


def attention_backward(qkv, gmix, mixed, stats, length, width, sums, between):
    rows = qkv.shape[0]
    half_rows = rows // 2
    lane = lax.broadcasted_iota(jnp.int32, (rows, LANES), 1)
    dead = key_bias(rows, length)
    zero = jnp.zeros((rows, LANES), bf16)
    one = jnp.ones((rows, LANES), bf16)
    for h in range(width // LANES):
        cols = [pl.ds(part * width + h * LANES, LANES) for part in range(3)]
        q2, k2, v2 = [qkv[:, c] for c in cols]
        g2 = gmix[:, cols[0]]
        terms = g2.astype(f32) * mixed[:, cols[0]].astype(f32)
        k2_t = k2.T
        grads_q, grads_k, grads_v = [], [], []
        for half in (0, 1):
            own = (lane < HEAD) if half == 0 else (lane >= HEAD)
            at = HEAD if half == 0 else 0
            delta = jnp.sum(jnp.where(own, terms, 0.0), axis=-1, keepdims=True)
            log_total = stats[:, 2 * h + half : 2 * h + half + 1]
            l0, l1, l2 = split_three(-log_total)
            d0, d1, d2 = split_three(-delta)
            m0, m1, m2, m3 = [lane == at + t for t in range(4)]
            m012 = m0 | m1 | m2
            qa = jnp.where(
                own,
                q2,
                jnp.where(m0, l0, jnp.where(m1, l1, jnp.where(m2, l2, jnp.where(m3, one, zero)))),
            )
            ga = jnp.where(own, g2, jnp.where(m0, d0, jnp.where(m1, d1, jnp.where(m2, d2, zero))))
            ka = jnp.where(own, k2, jnp.where(m012, one, jnp.where(m3, dead, zero)))
            va = jnp.where(own, v2, jnp.where(m012, one, zero))
            first = HEAD * half
            grad_q, parts_k, parts_v = None, [], []
            for block in (0, 1):
                low, high = block * half_rows, (block + 1) * half_rows
                probs = jnp.exp(mm(ka[low:high], qa, NT))
                grad_probs = mm(va[low:high], ga, NT)
                grad_scores = (probs * grad_probs).astype(bf16)
                parts_v.append(mm(probs.astype(bf16), g2))
                parts_k.append(mm(grad_scores, q2))
                term = mm(k2_t[first : first + HEAD, low:high], grad_scores)
                grad_q = term if grad_q is None else grad_q + term
            grads_q.append(grad_q)
            grads_k.append(jnp.concatenate(parts_k, 0))
            grads_v.append(jnp.concatenate(parts_v, 0))
        grad_q = jnp.concatenate(grads_q, 0).T * (HEAD ** -0.5)
        grad_k = jnp.where(lane < HEAD, grads_k[0], grads_k[1])
        grad_v = jnp.where(lane < HEAD, grads_v[0], grads_v[1])
        for c, grad in zip(cols, (grad_q, grad_k, grad_v)):
            qkv[:, c] = grad.astype(bf16)
        sums["bias_query"][:, cols[0]] += column_sum(grad_q)
        sums["bias_value"][:, cols[0]] += column_sum(grad_v)
        between(h)


def backward_block(grad_of, weights, vec, need, length, saved, work, sums, give, hook):
    w_qkv, w_out, w_in, w_back = weights
    qkv, mixed, stats, slope = saved
    unit, gouter, gatt, gmix, gsum = work
    rows, width = gsum.shape
    half_rows = rows // 2
    need("unit_ffn")

    def first(block, carry):
        rs = rows_at(block, half_rows)
        grad, unit_rows = grad_of(block), unit[rs, :]
        factor = stats[rs, FACTOR_FFN : FACTOR_FFN + 1]
        sums["gain_ffn"][...] += column_sum(grad * unit_rows)
        sums["shift_ffn"][...] += column_sum(grad)
        grad_sum = norm_back(grad * vec["gain_ffn"][...], unit_rows, factor)
        gsum[rs, :] = grad_sum
        gouter[rs, :] = grad_sum.astype(bf16)
        sums["bias_back"][...] += column_sum(grad_sum)
        return carry

    lax.fori_loop(0, 2, first, 0)
    hook("first", 0)
    need("hidden")

    def hidden(j, carry):
        cs = rows_at(j, width)
        grad_inner = mm(gouter[...], w_back[cs, :], NT) * slope[:, cs].astype(f32)
        sums["bias_in"](j)[...] += column_sum(grad_inner)
        slope[:, cs] = grad_inner.astype(bf16)
        hook("hidden", j)
        return carry

    lax.fori_loop(0, w_in.shape[1] // width, hidden, 0)
    hook("hidden_end", 0)
    need("middle")

    def middle(block, carry):
        rs = rows_at(block, half_rows)
        grad = gsum[rs, :] + mm(slope[rs, :], w_in[...], NT)
        unit_rows = unit[rs, :]
        factor = stats[rs, FACTOR_ATTN : FACTOR_ATTN + 1]
        sums["gain_attn"][...] += column_sum(grad * unit_rows)
        sums["shift_attn"][...] += column_sum(grad)
        grad_sum = norm_back(grad * vec["gain_attn"][...], unit_rows, factor)
        gsum[rs, :] = grad_sum
        rounded = grad_sum.astype(bf16)
        gatt[rs, :] = rounded
        sums["bias_out"][...] += column_sum(grad_sum)
        gmix[rs, :] = mm(rounded, w_out[...], NT).astype(bf16)
        hook("middle", block)
        return carry

    lax.fori_loop(0, 2, middle, 0)
    hook("middle_end", 0)
    need("attention")
    attention_backward(
        qkv, gmix, mixed, stats, length, width, sums, lambda h: hook("attention", h)
    )
    hook("attention_end", 0)
    need("last")

    def last(block, carry):
        rs = rows_at(block, half_rows)
        give(block, gsum[rs, :] + mm(qkv[rs, :], w_qkv[...], NT))
        hook("last", block)
        return carry

    lax.fori_loop(0, 2, last, 0)


def greet(partners):
    barrier = pltpu.get_barrier_semaphore()
    for partner in partners:
        pl.semaphore_signal(barrier, inc=1, device_id=partner, device_id_type=MESH)
    pl.semaphore_wait(barrier, len(partners))


def forward_kernel(*refs):
    (x_in, w_qkv, w_out, w_in, w_back), refs = refs[:5], refs[5:]
    vec, refs = dict(zip(FORWARD_VECTORS, refs)), refs[len(FORWARD_VECTORS) :]
    lengths, refs = refs[0], refs[1:]
    acts_out, x_out, refs = refs[0], refs[1], refs[2:]
    saved_out, refs = refs[:8], refs[8:]
    weights, refs = refs[:4], refs[4:]
    xbuf, result, refs = refs[0], refs[1], refs[2:]
    saved, refs = refs[:8], refs[8:]
    weight_sem, x_sem, send_sem, recv_sem, out_sem = refs
    rank = lax.axis_index("section")
    peer = (1 - rank, lax.axis_index("dp"))
    rows = xbuf.shape[1]
    half_rows = rows // 2
    loads = [
        pltpu.make_async_copy(source.at[0], target, weight_sem.at[i])
        for i, (source, target) in enumerate(zip((w_qkv, w_out, w_in, w_back), weights))
    ]

    def x_load(i):
        return pltpu.make_async_copy(x_in.at[rows_at(i, rows)], xbuf.at[i], x_sem.at[i])

    def handover(i, block):
        rs = rows_at(block, half_rows)
        return pltpu.make_async_remote_copy(
            src_ref=result.at[i, rs],
            dst_ref=xbuf.at[i, rs],
            send_sem=send_sem.at[i, block],
            recv_sem=recv_sem.at[i, block],
            device_id=peer,
            device_id_type=MESH,
        )

    @pl.when(rank == 0)
    def _():
        x_load(0).start()

    for load in loads:
        load.start()

    @pl.when(rank == 0)
    def _():
        x_load(1).start()

    greet([peer])

    def out_copy(i, k):
        source = (*saved, xbuf, result)[k]
        target = (*saved_out, x_out, acts_out)[k]
        return pltpu.make_async_copy(source.at[i], target.at[rows_at(i, rows)], out_sem.at[i, k])

    def micro_batch(i, carry):
        @pl.when(rank == 0)
        def _():
            x_load(i).wait()

        @pl.when(rank == 1)
        def _():
            handover(i, 0).wait_recv()
            handover(i, 1).wait_recv()

        def need(k):
            @pl.when(i == 0)
            def _():
                loads[k].wait()

        def send(block):
            @pl.when(rank == 0)
            def _():
                handover(i, block).start()

        def done(k):
            out_copy(i, k).start()

        done(8)
        forward_block(
            xbuf.at[i],
            weights,
            vec,
            need,
            lengths[i],
            [kept.at[i] for kept in saved],
            result.at[i],
            send,
            done,
        )
        return carry

    lax.fori_loop(0, MB, micro_batch, 0)

    def finish(i, carry):
        @pl.when(rank == 0)
        def _():
            handover(i, 0).wait_send()
            handover(i, 1).wait_send()

        for k in range(10):
            out_copy(i, k).wait()
        return carry

    lax.fori_loop(0, MB, finish, 0)


def backward_kernel(chips, *refs):
    (cotangent, w_qkv, w_out, w_in, w_back), refs = refs[:5], refs[5:]
    vec, refs = dict(gain_attn=refs[0], gain_ffn=refs[1]), refs[2:]
    lengths, refs = refs[0], refs[1:]
    qkv_in, mixed_in, stats_in, unit1_in, slope_in, unit2_in, active_in, normed_in, x_in = refs[:9]
    grad_out, blocks_out, sums_out, refs = refs[9], refs[10], refs[11], refs[12:]
    weights, refs = refs[:4], refs[4:]
    gbuf, qkv, mixed, stats, slope, unit, gouter, gatt, gmix, gsum, refs = *refs[:10], refs[10:]
    active, normed, x_kept, totals, total_slots, refs = *refs[:5], refs[5:]
    acc_first, away, sib, slots, refs = *refs[:4], refs[4:]
    weight_sem, g_sem, saved_sem, unit_sem, late_sem, send_sem, recv_sem, refs = *refs[:7], refs[7:]
    grad_sem, sib_send, sib_recv, sib_free, ring_send, ring_recv, refs = *refs[:6], refs[6:]
    share_send, share_recv, sum_send, sum_recv, out_sem, sum_out_sem = refs
    rank = lax.axis_index("section")
    me = lax.axis_index("dp")
    peer = (1 - rank, me)
    rows, width = gsum.shape
    half_rows = rows // 2

    core = lax.rem(me, 2)
    chip = lax.div(me, 2)
    ring_half = chips // 2
    place = jnp.where(lax.rem(chip, 2) == 0, lax.div(chip, 2), chips - 1 - lax.div(chip, 2))
    rounds, _, subs = ring_recv.shape[:3]
    piece = -(-width // (16 * subs * chips)) * 16 * subs
    part = piece // subs
    steps = chips - 1
    bits = total_slots.shape[0]

    def device_at(position):
        position = lax.rem(position + chips, chips)
        spot = jnp.where(position < ring_half, 2 * position, 2 * (chips - 1 - position) + 1)
        return (rank, 2 * spot + core)

    sibling = (rank, me + 1 - 2 * core)
    ways = (device_at(place + 1), device_at(place - 1))

    def across(bit):
        size = 1 << bit
        return (rank, me + size - 2 * size * lax.rem(lax.div(me, size), 2))

    w_loads = [
        pltpu.make_async_copy(source.at[0], target, weight_sem.at[i])
        for i, (source, target) in enumerate(zip((w_qkv, w_out, w_in, w_back), weights))
    ]
    late_loads = [
        pltpu.make_async_copy(source, target, late_sem.at[i])
        for i, (source, target) in enumerate(
            ((active_in, active), (normed_in, normed), (x_in, x_kept))
        )
    ]
    saved = (qkv, mixed, stats, slope)

    def g_load(i):
        rs = rows_at(i, rows)
        return pltpu.make_async_copy(cotangent.at[rs], gbuf.at[rs], g_sem.at[i])

    def saved_load(i, k):
        rs = rows_at(i, rows)
        source = (qkv_in, mixed_in, stats_in, slope_in)[k]
        return pltpu.make_async_copy(source.at[rs], saved[k].at[rs], saved_sem.at[i, k])

    def unit_load(i, k):
        source = (unit1_in, unit2_in)[k]
        return pltpu.make_async_copy(source.at[rows_at(i, rows)], unit, unit_sem.at[k])

    @pl.when(rank == 1)
    def _():
        g_load(0).start()

    unit_load(0, 1).start()
    saved_load(0, 2).start()
    w_loads[3].start()
    saved_load(0, 3).start()
    w_loads[2].start()
    w_loads[1].start()
    saved_load(0, 0).start()
    saved_load(0, 1).start()
    w_loads[0].start()

    @pl.when(rank == 1)
    def _():
        g_load(1).start()

    for k in (2, 3, 0, 1):
        saved_load(1, k).start()
    for load in late_loads:
        load.start()
    totals[...] = jnp.zeros_like(totals)
    sums = {name: totals.at[pl.ds(k, 1)] for k, name in enumerate(SUM_ROWS)}
    sums["bias_in"] = lambda j: totals.at[pl.ds(len(SUM_ROWS) + j, 1)]
    greet([peer, sibling, *ways] + [across(bit) for bit in range(1, bits)])

    def acc(r, way, rs=None):
        rs = pl.ds(0, width) if rs is None else rs
        if r == 0:
            return acc_first.at[way, rs]
        return weights[3].at[pl.ds(pl.multiple_of((2 * r - 2 + way) * width + rs.start, 16), rs.size)]

    def term(r, owner, way):
        j = 2 * owner + way
        cs = rows_at(j, width)
        if r == 0:
            return mm(active[:, cs], gouter[...], TN)
        if r == 1:
            return mm(normed[...], slope[:, cs], TN)
        raise ValueError

    def to_sibling(way):
        return pltpu.make_async_remote_copy(
            src_ref=away.at[way],
            dst_ref=sib.at[way],
            send_sem=sib_send.at[way],
            recv_sem=sib_recv.at[way],
            device_id=sibling,
            device_id_type=MESH,
        )

    def compute_into(r, owner, way, put):
        if r < 2:
            put(term(r, owner, way))
            return
        j = 2 * owner + way

        @pl.when(j == 0)
        def _():
            put(mm(mixed[...], gatt[...], TN))

        @pl.when(j > 0)
        def _():
            put(mm(x_kept[...], qkv[:, rows_at(jnp.maximum(j - 1, 0), width)], TN))

    def compute(r):
        late_loads[r].wait()
        if r > 0:
            pl.semaphore_wait(sib_free, 1)

        def for_sibling(way, carry):
            def put(value):
                away[way] = value.astype(bf16)

            compute_into(r, 1 - core, way, put)
            to_sibling(way).start()
            return carry

        lax.fori_loop(0, 2, for_sibling, 0)

        def for_me(way, carry):
            def put(value):
                acc(r, way)[...] = value.astype(bf16)

            compute_into(r, core, way, put)
            return carry

        lax.fori_loop(0, 2, for_me, 0)
        for way in (0, 1):
            to_sibling(way).wait()
            acc(r, way)[...] = (acc(r, way)[...].astype(f32) + sib[way].astype(f32)).astype(bf16)
        if r < rounds - 1:
            pl.semaphore_signal(sib_free, inc=1, device_id=sibling, device_id_type=MESH)

    def rows_of(way, sub, t):
        sign = 1 - 2 * way
        index = lax.rem(place - sign * t + 2 * chips, chips)
        return pl.ds(pl.multiple_of(index * piece + sub * part, 16), part)

    def ring(r, way, sub, t, target):
        return pltpu.make_async_remote_copy(
            src_ref=acc(r, way, rows_of(way, sub, t)),
            dst_ref=target,
            send_sem=ring_send.at[r, way, sub, lax.rem(t, 2)],
            recv_sem=ring_recv.at[r, way, sub, t],
            device_id=ways[way],
            device_id_type=MESH,
        )

    def adding(r, way, sub, t):
        return ring(r, way, sub, t, slots.at[r, way, rows_of(way, sub, t)])

    def handing(r, way, sub, t):
        return ring(r, way, sub, t, acc(r, way, rows_of(way, sub, t)))

    def share(r, way, rs):
        return pltpu.make_async_remote_copy(
            src_ref=acc(r, way, rs),
            dst_ref=blocks_out.at[4 * r + 2 * core + way, rs],
            send_sem=share_send.at[r, way],
            recv_sem=share_recv.at[r, way],
            device_id=sibling,
            device_id_type=MESH,
        )

    def place_out(r, way, rs):
        block = blocks_out.at[4 * r + 2 * core + way, rs]
        return pltpu.make_async_copy(acc(r, way, rs), block, out_sem.at[r, way])

    def when(condition, way, t, body):
        if chips * piece > width:
            condition = condition & (rows_of(way, 0, t).start < width)
        if condition is True:
            body()
        elif condition is not False:
            pl.when(condition)(body)

    def chain(r, way, sub, t):
        def sent():
            adding(r, way, sub, t - 2).wait_send()

        def added():
            adding(r, way, sub, t - 1).wait_recv()
            rs = rows_of(way, sub, t)
            acc(r, way, rs)[...] = (
                acc(r, way, rs)[...].astype(f32) + slots[r, way, rs].astype(f32)
            ).astype(bf16)

        def kept():
            handing(r, way, sub, t - 1).wait_recv()

        def whole():
            share(r, way, rows_of(way, sub, t)).start()
            place_out(r, way, rows_of(way, sub, t)).start()

        when((t >= 2) & (t <= 2 * steps + 1), way, t - 2, sent)
        when((t >= 1) & (t <= steps), way, t, added)
        when((t >= 0) & (t < steps), way, t, lambda: adding(r, way, sub, t).start())
        when((t > steps) & (t <= 2 * steps), way, t, kept)
        when((t >= steps) & (t < 2 * steps), way, t, lambda: handing(r, way, sub, t).start())
        when((t >= steps) & (t <= 2 * steps), way, t, whole)

    def slot(tick, offsets):
        for r, offset in enumerate(offsets):
            for sub in range(subs):
                for way in (0, 1):
                    chain(r, way, sub, tick - offset)

    def handover(i, block):
        rs = rows_at(block, half_rows)
        target = gbuf.at[pl.ds(pl.multiple_of(i * rows + block * half_rows, half_rows), half_rows)]
        return pltpu.make_async_remote_copy(
            src_ref=gmix.at[rs],
            dst_ref=target,
            send_sem=send_sem.at[block],
            recv_sem=recv_sem.at[i, block],
            device_id=peer,
            device_id_type=MESH,
        )

    def grad_copy(i, block):
        target = grad_out.at[pl.ds(pl.multiple_of(i * rows + block * half_rows, half_rows), half_rows)]
        return pltpu.make_async_copy(gsum.at[rows_at(block, half_rows)], target, grad_sem.at[block])

    early = (0, 4, 10)

    def micro_batch(i, carry):
        mine = rows_at(i, rows)

        def need(what):
            if what == "unit_ffn":
                unit_load(i, 1).wait()
                saved_load(i, 2).wait()

                @pl.when(rank == 1)
                def _():
                    g_load(i).wait()

                @pl.when(i > 0)
                def _():
                    for block in (0, 1):
                        grad_copy(0, block).wait()

            if what == "hidden":
                unit_load(i, 0).start()
                saved_load(i, 3).wait()
            if what == "middle":
                unit_load(i, 0).wait()

                @pl.when((i > 0) & (rank == 1))
                def _():
                    for block in (0, 1):
                        handover(0, block).wait_send()

            if what == "attention":

                @pl.when(i < MB - 1)
                def _():
                    unit_load(i + 1, 1).start()

                saved_load(i, 0).wait()
                saved_load(i, 1).wait()

            @pl.when(i == 0)
            def _():
                for load in dict(hidden=(3,), middle=(2, 1), last=(0,)).get(what, ()):
                    w_loads[load].wait()

        def hook(what, k):
            now = (i == MB - 1) & (rank == 0)

            def at(condition, body):
                pl.when(now & condition)(body)

            if what == "first":

                @pl.when(now)
                def _():
                    compute(0)
                    slot(0, early[:1])

            if what == "hidden":
                at(k == 1, lambda: slot(1, early[:1]))
                at(k == 3, lambda: slot(2, early[:1]))
            if what == "hidden_end":

                @pl.when(now)
                def _():
                    compute(1)
                    slot(3, early[:1])
                    slot(4, early[:2])

            if what == "middle":
                at(k == 0, lambda: slot(5, early[:2]))
                at(k == 1, lambda: slot(6, early[:2]))
            if what == "attention" and k % 2 == 1:

                @pl.when(now)
                def _():
                    slot(7 + k // 2, early[:2])

            if what == "attention_end":

                @pl.when(now)
                def _():
                    compute(2)
                    slot(10, early)

            if what == "last":
                at(k == 0, lambda: slot(11, early))
                at(k == 1, lambda: slot(12, early))

        def grad_of(block):
            @pl.when(rank == 0)
            def _():
                handover(i, block).wait_recv()

            rs = pl.ds(pl.multiple_of(i * rows + block * half_rows, half_rows), half_rows)
            return gbuf[rs, :].astype(f32)

        def give(block, value):
            rs = rows_at(block, half_rows)
            rounded = value.astype(bf16)
            gmix[rs, :] = rounded
            gsum[rs, :] = jnp.where(rank == 1, rounded.astype(f32), value)
            grad_copy(i, block).start()

            @pl.when(rank == 1)
            def _():
                handover(i, block).start()

        backward_block(
            grad_of,
            weights,
            vec,
            need,
            lengths[i],
            [kept.at[mine] for kept in saved],
            (unit, gouter.at[mine], gatt.at[mine], gmix, gsum),
            sums,
            give,
            hook,
        )
        return carry

    lax.fori_loop(0, MB, micro_batch, 0)

    def sum_step(bit):
        return pltpu.make_async_remote_copy(
            src_ref=totals,
            dst_ref=total_slots.at[bit],
            send_sem=sum_send.at[bit],
            recv_sem=sum_recv.at[bit],
            device_id=across(bit),
            device_id_type=MESH,
        )

    @pl.when(rank == 1)
    def _():
        compute(0)

    start = jnp.where(rank == 0, 13, 0)
    offsets = [jnp.where(rank == 0, early[r], r) for r in range(rounds)]

    def rest(tick, carry):
        slot(tick, offsets)
        for r in range(1, rounds):

            @pl.when((rank == 1) & (tick == r - 1))
            def _():
                compute(r)

        for bit in range(bits + 1):

            @pl.when(tick - start == 2 + bit)
            def _():
                if bit > 0:
                    sum_step(bit - 1).wait()
                    totals[...] += total_slots[bit - 1]
                if bit < bits:
                    sum_step(bit).start()

        return carry

    lax.fori_loop(start, offsets[-1] + 2 * steps + 2, rest, 0)
    sum_copy = pltpu.make_async_copy(totals, sums_out, sum_out_sem)
    sum_copy.start()
    for block in (0, 1):
        grad_copy(MB - 1, block).wait()

        @pl.when(rank == 1)
        def _():
            handover(MB - 1, block).wait_send()

    everything = pl.ds(0, width)
    for r in range(rounds):
        for way in (0, 1):
            share(r, way, everything).wait_recv()
            share(r, way, everything).wait_send()
            place_out(r, way, everything).wait()
    sum_copy.wait()


def finish_kernel(blocks, sums, *outs):
    step = pl.program_id(0)
    grads, vectors = outs[:4], outs[4:]
    width = sums.shape[1]
    value = blocks[0].astype(f32)
    for k, (low, high) in enumerate(((0, 4), (4, 8), (8, 9), (9, 12))):

        @pl.when((step >= low) & (step < high))
        def _():
            grads[k][0] = value

    @pl.when(step == 0)
    def _():
        for k, out in enumerate(vectors[:-1]):
            out[...] = sums[k : k + 1, :]
        for j in range(vectors[-1].shape[1] // width):
            row = len(vectors) - 1 + j
            vectors[-1][:, j * width : (j + 1) * width] = sums[row : row + 1, :]


def per_device(chips, *args):
    x_input = args[0]
    names = (
        "w_qkv", "bias_query", "bias_value", "w_out", "bias_out", "gain_attn", "shift_attn",
        "w_in", "bias_in", "w_back", "bias_back", "gain_ffn", "shift_ffn",
    )
    given = dict(zip(names, args[1:14]))
    lengths, cotangent = args[14:]
    row_count, width = x_input.shape
    rows = row_count // MB
    hidden = given["w_in"].shape[2]
    weights = [given[name] for name in ("w_qkv", "w_out", "w_in", "w_back")]
    anywhere = pl.BlockSpec(memory_space=pl.ANY)
    vmem = pl.BlockSpec(memory_space=pltpu.VMEM)
    smem = pl.BlockSpec(memory_space=pltpu.SMEM)
    dma = pltpu.SemaphoreType.DMA
    shape = jax.ShapeDtypeStruct
    weight_scratch = [pltpu.VMEM(w.shape[1:], bf16) for w in weights]
    kept = [
        (3 * width, bf16),
        (width, bf16),
        (LANES, f32),
        (width, f32),
        (width, bf16),
        (hidden, bf16),
        (hidden, bf16),
        (width, f32),
    ]

    def buffers(columns):
        return [pltpu.VMEM((MB, rows, n), kind) for n, kind in columns]

    acts, x_kept, *saved = pl.pallas_call(
        forward_kernel,
        out_shape=[shape((row_count, width), bf16)] * 2
        + [shape((row_count, n), kind) for n, kind in kept],
        in_specs=[anywhere] * 5 + [vmem] * len(FORWARD_VECTORS) + [smem],
        out_specs=[anywhere] * 10,
        scratch_shapes=weight_scratch
        + buffers([(width, bf16)] * 2 + kept)
        + [dma((4,)), dma((MB,)), dma((MB, 2)), dma((MB, 2)), dma((MB, 10))],
        compiler_params=pltpu.CompilerParams(
            collective_id=0, has_side_effects=True, vmem_limit_bytes=VMEM_LIMIT
        ),
        name="forward",
    )(x_input, *weights, *[given[name] for name in FORWARD_VECTORS], lengths)
    qkv, mixed, stats, unit1, normed, active, slope, unit2 = saved
    rounds = (3 * width + width + 2 * hidden) // (4 * width)
    subs = 2 if width % (32 * chips) == 0 else 1
    steps = chips - 1
    bits = (2 * chips).bit_length() - 1

    def whole_rows(columns):
        return [pltpu.VMEM((row_count, n), kind) for n, kind in columns]

    square = (width, width)
    input_grads, blocks, totals = pl.pallas_call(
        functools.partial(backward_kernel, chips),
        out_shape=[
            shape((row_count, width), f32),
            shape((4 * rounds, *square), bf16),
            shape((SUM_COUNT, width), f32),
        ],
        in_specs=[anywhere] * 5 + [vmem] * 2 + [smem] + [anywhere] * 9,
        out_specs=[anywhere] * 3,
        scratch_shapes=weight_scratch
        + whole_rows([(width, bf16), kept[0], kept[1], kept[2], kept[6]])
        + [pltpu.VMEM((rows, width), f32)]
        + whole_rows([(width, bf16)] * 2)
        + [pltpu.VMEM((rows, width), bf16), pltpu.VMEM((rows, width), f32)]
        + whole_rows([(hidden, bf16), (width, bf16), (width, bf16)])
        + [
            pltpu.VMEM((SUM_COUNT, width), f32),
            pltpu.VMEM((bits, SUM_COUNT, width), f32),
            pltpu.VMEM((2, *square), bf16),
            pltpu.VMEM((2, *square), bf16),
            pltpu.VMEM((2, *square), bf16),
            pltpu.VMEM((rounds, 2, *square), bf16),
            dma((4,)),
            dma((MB,)),
            dma((MB, 4)),
            dma((2,)),
            dma((3,)),
            dma((2,)),
            dma((MB, 2)),
            dma((2,)),
            dma((2,)),
            dma((2,)),
            pltpu.SemaphoreType.REGULAR,
            dma((rounds, 2, subs, 2)),
            dma((rounds, 2, subs, 2 * steps)),
            dma((rounds, 2)),
            dma((rounds, 2)),
            dma((bits,)),
            dma((bits,)),
            dma((rounds, 2)),
            dma,
        ],
        compiler_params=pltpu.CompilerParams(
            collective_id=1, has_side_effects=True, vmem_limit_bytes=VMEM_LIMIT
        ),
        name="backward",
    )(
        cotangent, *weights, given["gain_attn"], given["gain_ffn"], lengths,
        qkv, mixed, stats, unit1, slope, unit2, active, normed, x_kept,
    )

    def square_of(low, high, index):
        def index_map(step):
            return index(jnp.clip(step - low, 0, high - low - 1))

        return pl.BlockSpec((1, width, width), index_map)

    vector_names = SUM_ROWS + ("bias_in",)
    whole = pl.pallas_call(
        finish_kernel,
        grid=(4 * rounds,),
        out_shape=[
            shape((1, hidden, width), f32),
            shape((1, width, hidden), f32),
            shape((1, width, width), f32),
            shape((1, width, 3 * width), f32),
        ]
        + [shape(given[name].shape, f32) for name in vector_names],
        in_specs=[
            pl.BlockSpec((1, width, width), lambda step: (step, 0, 0)),
            pl.BlockSpec((SUM_COUNT, width), lambda step: (0, 0)),
        ],
        out_specs=[
            square_of(0, 4, lambda j: (0, j, 0)),
            square_of(4, 8, lambda j: (0, 0, j)),
            square_of(8, 9, lambda j: (0, 0, 0)),
            square_of(9, 12, lambda j: (0, 0, j)),
        ]
        + [pl.BlockSpec(given[name].shape, lambda step: (0, 0)) for name in vector_names],
        compiler_params=pltpu.CompilerParams(vmem_limit_bytes=VMEM_LIMIT),
        name="finish",
    )(blocks, totals)
    grads = dict(zip(("w_back", "w_in", "w_out", "w_qkv") + vector_names, whole))
    return (acts[None], input_grads[None], *[grads[name] for name in names])


def solution(mesh):
    return jax.shard_map(
        functools.partial(per_device, mesh.shape["dp"] // 2),
        mesh=mesh,
        in_specs=(
            P("dp", None),
            P("section", None, None),
            P("section", None),
            P("section", None),
            P("section", None, None),
            P("section", None),
            P("section", None),
            P("section", None),
            P("section", None, None),
            P("section", None),
            P("section", None, None),
            P("section", None),
            P("section", None),
            P("section", None),
            P("dp"),
            P("dp", None),
        ),
        out_specs=(
            P("section", "dp", None),
            P("section", "dp", None),
            P("section", None, None),
            P("section", None),
            P("section", None),
            P("section", None, None),
            P("section", None),
            P("section", None),
            P("section", None),
            P("section", None, None),
            P("section", None),
            P("section", None, None),
            P("section", None),
            P("section", None),
            P("section", None),
        ),
        check_vma=False,
    )
```

```python
import functools

import jax
import jax.numpy as jnp
from jax import lax
from jax.experimental import pallas as pl
from jax.experimental.pallas import tpu as pltpu
from jax.sharding import PartitionSpec as P

HEAD = 64
LANES = 128
MB = 2
EPSILON = 1e-12
DEAD = -1e30
FACTOR_ATTN = 12
FACTOR_FFN = 13
STAT_COLUMNS = 16
VMEM_LIMIT = 62 << 20

FORWARD_VECTORS = (
    "bias_query",
    "bias_value",
    "bias_out",
    "gain_attn",
    "shift_attn",
    "bias_in",
    "bias_back",
    "gain_ffn",
    "shift_ffn",
)
SUM_ROWS = tuple(name for name in FORWARD_VECTORS if name != "bias_in")
SUM_COUNT = 16

f32 = jnp.float32
bf16 = jnp.bfloat16
MESH = pl.DeviceIdType.MESH
NN = (((1,), (0,)), ((), ()))
NT = (((1,), (1,)), ((), ()))
TN = (((0,), (0,)), ((), ()))


def mm(left, right, dims=NN):
    return lax.dot_general(left, right, dims, preferred_element_type=f32)


def rows_at(index, count):
    return pl.ds(pl.multiple_of(index * count, count), count)


def norm_rows(value):
    centred = value - jnp.mean(value, axis=-1, keepdims=True)
    factor = lax.rsqrt(jnp.mean(centred * centred, axis=-1, keepdims=True) + EPSILON)
    return centred * factor, factor


def norm_back(grad_hat, unit, factor):
    return factor * (
        grad_hat
        - jnp.mean(grad_hat, axis=-1, keepdims=True)
        - unit * jnp.mean(grad_hat * unit, axis=-1, keepdims=True)
    )


def column_sum(value):
    return jnp.sum(value, axis=0, keepdims=True)


def split_three(value):
    high = value.astype(bf16)
    rest = value - high.astype(f32)
    middle = rest.astype(bf16)
    low = (rest - middle.astype(f32)).astype(bf16)
    return high, middle, low


def key_bias(rows, length):
    key = lax.broadcasted_iota(jnp.int32, (rows, LANES), 0)
    return jnp.where(key < length, 0.0, DEAD).astype(bf16)


def attention_forward(qkv, mixed, stats, length, width):
    rows = qkv.shape[0]
    heads = width // HEAD
    lane = lax.broadcasted_iota(jnp.int32, (rows, LANES), 1)
    dead = key_bias(rows, length)
    zero = jnp.zeros((rows, LANES), bf16)
    one = jnp.ones((rows, LANES), bf16)

    def marked(part, head, mark):
        value = qkv[:, pl.ds(part * width + head // 2 * LANES, LANES)]
        own = (lane < HEAD) if head % 2 == 0 else (lane >= HEAD)
        return jnp.where(own, value, jnp.where(lane == HEAD - HEAD * (head % 2), mark, zero))

    def scores_of(head):
        return mm(marked(1, head, dead), marked(0, head, one), NT)

    ahead = [scores_of(0), scores_of(1)]
    outs, log_totals = [], []
    for head in range(heads):
        if head + 2 < heads:
            ahead.append(scores_of(head + 2))
        scores = ahead[head]
        ahead[head] = None
        highest = jnp.max(scores, axis=0, keepdims=True)
        weights = jnp.exp(scores - highest).astype(bf16)
        product = mm(marked(2, head, one).T, weights)
        odd = head % 2
        total = product[HEAD - HEAD * odd : HEAD - HEAD * odd + 1]
        outs.append(product[HEAD * odd : HEAD * odd + HEAD] * (1.0 / total))
        log_totals.append(highest + jnp.log(total))
        if odd:
            mixed[:, pl.ds(head // 2 * LANES, LANES)] = jnp.concatenate(outs, 0).T.astype(bf16)
            outs = []
    spare = STAT_COLUMNS - heads
    log_totals = jnp.concatenate(log_totals + [jnp.zeros((spare, rows), f32)], 0)
    stats[:, :STAT_COLUMNS] = log_totals.T


def forward_block(weights, vec, need, length, saved, unit1, unit2, result, send, done):
    w_qkv, w_out, w_in, w_back = weights
    x, qkv, mixed, stats, slope, active, normed = saved
    rows, width = x.shape
    half_rows = rows // 2
    scale = HEAD ** -0.5
    need("query")
    qkv[:, :width] = ((mm(x[...], w_qkv[:, :width]) + vec["bias_query"][...]) * scale).astype(bf16)
    need("key")
    qkv[:, width : 2 * width] = mm(x[...], w_qkv[:, width : 2 * width]).astype(bf16)
    qkv[:, 2 * width :] = (mm(x[...], w_qkv[:, 2 * width :]) + vec["bias_value"][...]).astype(bf16)
    attention_forward(qkv, mixed, stats, length, width)
    lane = lax.broadcasted_iota(jnp.int32, (half_rows, LANES), 1)
    need("out")

    def after_attention(block, carry):
        rs = rows_at(block, half_rows)
        summed = x[rs, :].astype(f32) + mm(mixed[rs, :], w_out[...]) + vec["bias_out"][...]
        unit, factor = norm_rows(summed)
        unit1[rs, :] = unit
        normed[rs, :] = (unit * vec["gain_attn"][...] + vec["shift_attn"][...]).astype(bf16)
        stats[rs, :] = jnp.where(lane == FACTOR_ATTN, factor, stats[rs, :])
        return carry

    lax.fori_loop(0, 2, after_attention, 0)
    done("attn")
    need("in")

    def hidden(j, carry):
        cs = rows_at(j, width)
        inner = mm(normed[...], w_in[:, cs]) + vec["bias_in"][:, cs]
        share = 0.5 * (1.0 + lax.erf(inner * 0.7071067811865476))
        active[:, cs] = (inner * share).astype(bf16)
        slope[:, cs] = (
            share + inner * jnp.exp(-0.5 * inner * inner) * 0.3989422804014327
        ).astype(bf16)
        return carry

    lax.fori_loop(0, w_in.shape[1] // width, hidden, 0)
    need("back")

    def after_ffn(block, carry):
        rs = rows_at(block, half_rows)
        summed = normed[rs, :].astype(f32) + mm(active[rs, :], w_back[...]) + vec["bias_back"][...]
        unit, factor = norm_rows(summed)
        unit2[rs, :] = unit
        result[rs, :] = (unit * vec["gain_ffn"][...] + vec["shift_ffn"][...]).astype(bf16)
        stats[rs, :] = jnp.where(lane == FACTOR_FFN, factor, stats[rs, :])
        send(block)
        return carry

    lax.fori_loop(0, 2, after_ffn, 0)
    done("ffn")


def attention_backward(qkv, gmix, mixed, stats, length, width, sums, between):
    rows = qkv.shape[0]
    heads = width // HEAD
    lane = lax.broadcasted_iota(jnp.int32, (rows, LANES), 1)
    dead = key_bias(rows, length)
    zero = jnp.zeros((rows, LANES), bf16)
    one = jnp.ones((rows, LANES), bf16)

    def operands(head):
        cols = [pl.ds(part * width + head // 2 * LANES, LANES) for part in range(3)]
        q2, k2, v2 = [qkv[:, c] for c in cols]
        g2 = gmix[:, cols[0]]
        own = (lane < HEAD) if head % 2 == 0 else (lane >= HEAD)
        at = HEAD - HEAD * (head % 2)
        terms = jnp.where(own, g2.astype(f32) * mixed[:, cols[0]].astype(f32), 0.0)
        d0, d1, d2 = split_three(-jnp.sum(terms, axis=-1, keepdims=True))
        l0, l1, l2 = split_three(-stats[:, head : head + 1])
        m0, m1, m2, m3 = [lane == at + t for t in range(4)]
        m012 = m0 | m1 | m2
        qa = jnp.where(
            own,
            q2,
            jnp.where(m0, l0, jnp.where(m1, l1, jnp.where(m2, l2, jnp.where(m3, one, zero)))),
        )
        ga = jnp.where(own, g2, jnp.where(m0, d0, jnp.where(m1, d1, jnp.where(m2, d2, zero))))
        ka = jnp.where(own, k2, jnp.where(m012, one, jnp.where(m3, dead, zero)))
        va = jnp.where(own, v2, jnp.where(m012, one, zero))
        first = HEAD * (head % 2)
        return q2, g2, k2.T[first : first + HEAD], mm(ka, qa, NT), mm(va, ga, NT)

    ahead = operands(0)
    grads = []
    for head in range(heads):
        q2, g2, k2_t, scores, grad_probs = ahead
        if head + 1 < heads:
            ahead = operands(head + 1)
        probs = jnp.exp(scores)
        grad_scores = (probs * grad_probs).astype(bf16)
        grads.append((mm(k2_t, grad_scores), mm(grad_scores, q2), mm(probs.astype(bf16), g2)))
        if head % 2:
            pair = head // 2
            even, odd = grads
            grads = []
            grad_q = jnp.concatenate([even[0], odd[0]], 0).T * (HEAD ** -0.5)
            grad_k = jnp.where(lane < HEAD, even[1], odd[1])
            grad_v = jnp.where(lane < HEAD, even[2], odd[2])
            for part, grad in enumerate((grad_q, grad_k, grad_v)):
                qkv[:, pl.ds(part * width + pair * LANES, LANES)] = grad.astype(bf16)
            cols = pl.ds(pair * LANES, LANES)
            sums["bias_query"][:, cols] += column_sum(grad_q)
            sums["bias_value"][:, cols] += column_sum(grad_v)
            between(pair)


def backward_block(grad_of, unit_of, weights, vec, need, length, saved, work, sums, give, hook):
    w_qkv, w_out, w_in, w_back = weights
    qkv, mixed, stats, slope = saved
    unit, gouter, gatt, gmix, gsum = work
    rows, width = gsum.shape
    half_rows = rows // 2
    need("unit_ffn")

    def first(block, carry):
        rs = rows_at(block, half_rows)
        grad, unit_rows = grad_of(block), unit_of(block)
        factor = stats[rs, FACTOR_FFN : FACTOR_FFN + 1]
        sums["gain_ffn"][...] += column_sum(grad * unit_rows)
        sums["shift_ffn"][...] += column_sum(grad)
        grad_sum = norm_back(grad * vec["gain_ffn"][...], unit_rows, factor)
        gsum[rs, :] = grad_sum
        gouter[rs, :] = grad_sum.astype(bf16)
        sums["bias_back"][...] += column_sum(grad_sum)
        return carry

    lax.fori_loop(0, 2, first, 0)
    hook("first", 0)
    need("hidden")

    def hidden(j, carry):
        cs = rows_at(j, width)
        grad_inner = mm(gouter[...], w_back[cs, :], NT) * slope[:, cs].astype(f32)
        sums["bias_in"](j)[...] += column_sum(grad_inner)
        slope[:, cs] = grad_inner.astype(bf16)
        hook("hidden", j)
        return carry

    lax.fori_loop(0, w_in.shape[1] // width, hidden, 0)
    hook("hidden_end", 0)
    need("middle")

    def middle(block, carry):
        rs = rows_at(block, half_rows)
        grad = gsum[rs, :] + mm(slope[rs, :], w_in[...], NT)
        unit_rows = unit[rs, :]
        factor = stats[rs, FACTOR_ATTN : FACTOR_ATTN + 1]
        sums["gain_attn"][...] += column_sum(grad * unit_rows)
        sums["shift_attn"][...] += column_sum(grad)
        grad_sum = norm_back(grad * vec["gain_attn"][...], unit_rows, factor)
        gsum[rs, :] = grad_sum
        rounded = grad_sum.astype(bf16)
        gatt[rs, :] = rounded
        sums["bias_out"][...] += column_sum(grad_sum)
        gmix[rs, :] = mm(rounded, w_out[...], NT).astype(bf16)
        hook("middle", block)
        return carry

    lax.fori_loop(0, 2, middle, 0)
    hook("middle_end", 0)
    need("attention")
    attention_backward(
        qkv, gmix, mixed, stats, length, width, sums, lambda h: hook("attention", h)
    )
    hook("attention_end", 0)
    need("last")

    def last(block, carry):
        rs = rows_at(block, half_rows)
        give(block, gsum[rs, :] + mm(qkv[rs, :], w_qkv[...], NT))
        hook("last", block)
        return carry

    lax.fori_loop(0, 2, last, 0)


def layer_kernel(chips, *refs):
    (x_in, cotangent, w_qkv, w_out, w_in, w_back), refs = refs[:6], refs[6:]
    vec, refs = dict(zip(FORWARD_VECTORS, refs)), refs[len(FORWARD_VECTORS) :]
    lengths, refs = refs[0], refs[1:]
    acts_out, grad_out, blocks_out, sums_out, units_out, refs = *refs[:5], refs[5:]
    weights, refs = refs[:4], refs[4:]
    x_kept, qkv, mixed, stats, slope, active, normed, refs = *refs[:7], refs[7:]
    gouter, gatt, gmix, gsend, gsum, unit, totals, total_slots, refs = *refs[:8], refs[8:]
    acc_first, slots, refs = *refs[:2], refs[2:]
    weight_sem, x_sem, g_sem, unit_sem, acts_sem, forth_send, forth_recv, refs = *refs[:7], refs[7:]
    back_send, back_recv, grad_sem, sib_send, sib_recv, sib_free, refs = *refs[:6], refs[6:]
    ring_send, ring_recv, share_send, share_recv, sum_send, sum_recv, refs = *refs[:6], refs[6:]
    out_sem, sum_out_sem = refs
    rank = lax.axis_index("section")
    me = lax.axis_index("dp")
    peer = (1 - rank, me)
    rows, width = gsum.shape
    half_rows = rows // 2

    core = lax.rem(me, 2)
    chip = lax.div(me, 2)
    ring_half = chips // 2
    place = jnp.where(lax.rem(chip, 2) == 0, lax.div(chip, 2), chips - 1 - lax.div(chip, 2))
    rounds, _, subs = ring_recv.shape[:3]
    piece = -(-width // (16 * subs * chips)) * 16 * subs
    part = piece // subs
    steps = chips - 1
    bits = total_slots.shape[0]

    def device_at(position):
        position = lax.rem(position + chips, chips)
        spot = jnp.where(position < ring_half, 2 * position, 2 * (chips - 1 - position) + 1)
        return (rank, 2 * spot + core)

    sibling = (rank, me + 1 - 2 * core)
    ways = (device_at(place + 1), device_at(place - 1))

    def across(bit):
        size = 1 << bit
        return (rank, me + size - 2 * size * lax.rem(lax.div(me, size), 2))

    def half_at(i, block):
        return pl.ds(pl.multiple_of(i * rows + block * half_rows, half_rows), half_rows)

    query = pl.ds(0, width)
    key_value = pl.ds(width, 2 * width)
    loads = dict(
        query=(w_qkv.at[0, :, query], weights[0].at[:, query]),
        key=(w_qkv.at[0, :, key_value], weights[0].at[:, key_value]),
        out=(w_out.at[0], weights[1]),
        back=(w_back.at[0], weights[3]),
    )
    loads["in"] = (w_in.at[0], weights[2])
    order = ("query", "key", "out", "in", "back")
    loads = {
        name: pltpu.make_async_copy(*loads[name], weight_sem.at[k]) for k, name in enumerate(order)
    }

    def x_load(i):
        rs = rows_at(i, rows)
        return pltpu.make_async_copy(x_in.at[rs], x_kept.at[rs], x_sem.at[i])

    def g_load():
        return pltpu.make_async_copy(cotangent, gouter, g_sem)

    @pl.when(rank == 0)
    def _():
        x_load(0).start()

    loads["query"].start()
    loads["key"].start()
    barrier = pltpu.get_barrier_semaphore()
    partners = [peer, sibling, *ways] + [across(bit) for bit in range(1, bits)]
    for partner in partners:
        pl.semaphore_signal(barrier, inc=1, device_id=partner, device_id_type=MESH)
    totals[...] = jnp.zeros_like(totals)
    sums = {name: totals.at[pl.ds(k, 1)] for k, name in enumerate(SUM_ROWS)}
    sums["bias_in"] = lambda j: totals.at[pl.ds(len(SUM_ROWS) + j, 1)]
    pl.semaphore_wait(barrier, len(partners))

    def forth(i, block):
        rs = half_at(i, block)
        return pltpu.make_async_remote_copy(
            src_ref=gatt.at[rs],
            dst_ref=x_kept.at[rs],
            send_sem=forth_send.at[i, block],
            recv_sem=forth_recv.at[i, block],
            device_id=peer,
            device_id_type=MESH,
        )

    def acts_copy(i):
        rs = rows_at(i, rows)
        return pltpu.make_async_copy(gatt.at[rs], acts_out.at[rs], acts_sem.at[i])

    def spill(k):
        return pltpu.make_async_copy((unit, gsum)[k], units_out.at[k], unit_sem.at[k])

    def unspill(k):
        return pltpu.make_async_copy(units_out.at[k], unit, unit_sem.at[k])

    def forward_batch(i, carry):
        mine = rows_at(i, rows)

        @pl.when(rank == 0)
        def _():
            x_load(i).wait()

        @pl.when(rank == 1)
        def _():
            forth(i, 0).wait_recv()
            forth(i, 1).wait_recv()

        def need(what):
            @pl.when(i == 0)
            def _():
                loads[what].wait()
                if what == "key":
                    loads["out"].start()
                    loads["in"].start()
                if what == "out":
                    loads["back"].start()

                    @pl.when(rank == 0)
                    def _():
                        x_load(1).start()

                    @pl.when(rank == 1)
                    def _():
                        g_load().start()

            if what in ("out", "back"):

                @pl.when(i > 0)
                def _():
                    spill(0 if what == "out" else 1).wait()

        def done(what):
            @pl.when(i < MB - 1)
            def _():
                spill(0 if what == "attn" else 1).start()

            if what == "ffn":
                acts_copy(i).start()

        def send(block):
            @pl.when(rank == 0)
            def _():
                forth(i, block).start()

        forward_block(
            weights,
            vec,
            need,
            lengths[i],
            [ref.at[mine] for ref in (x_kept, qkv, mixed, stats, slope, active, normed)],
            unit,
            gsum,
            gatt.at[mine],
            send,
            done,
        )
        return carry

    lax.fori_loop(0, MB, forward_batch, 0)

    def acc(r, way, rs=None):
        rs = pl.ds(0, width) if rs is None else rs
        if r == 0:
            return acc_first.at[way, rs]
        return weights[3].at[pl.ds(pl.multiple_of((2 * r - 2 + way) * width + rs.start, 16), rs.size)]

    def term(r, owner, way):
        j = 2 * owner + way
        cs = rows_at(j, width)
        if r == 0:
            return mm(active[:, cs], gouter[...], TN)
        return mm(normed[...], slope[:, cs], TN)

    def sibling_term(r, way):
        if r == 0:
            return slots.at[1, way]
        return active.at[pl.ds(0, width), rows_at(way, width)]

    def to_sibling(r, way):
        return pltpu.make_async_remote_copy(
            src_ref=acc(r, way),
            dst_ref=sibling_term(r, way),
            send_sem=sib_send.at[way],
            recv_sem=sib_recv.at[way],
            device_id=sibling,
            device_id_type=MESH,
        )

    def compute_into(r, owner, way, put):
        if r < 2:
            put(term(r, owner, way))
            return
        j = 2 * owner + way

        @pl.when(j == 0)
        def _():
            put(mm(mixed[...], gatt[...], TN))

        @pl.when(j > 0)
        def _():
            put(mm(x_kept[...], qkv[:, rows_at(jnp.maximum(j - 1, 0), width)], TN))

    def compute(r, between=lambda: None):
        if r > 0:
            pl.semaphore_wait(sib_free, 1)

        def for_sibling(way, carry):
            def put(value):
                acc(r, way)[...] = value.astype(bf16)

            compute_into(r, 1 - core, way, put)
            to_sibling(r, way).start()
            return carry

        lax.fori_loop(0, 2, for_sibling, 0)
        between()

        def for_me(way, carry):
            def put(value):
                acc(r, way)[...] = value.astype(bf16)

            to_sibling(r, way).wait_send()
            compute_into(r, core, way, put)
            return carry

        lax.fori_loop(0, 2, for_me, 0)
        for way in (0, 1):
            to_sibling(r, way).wait_recv()
            acc(r, way)[...] = (acc(r, way)[...].astype(f32) + sibling_term(r, way)[...].astype(f32)).astype(bf16)
        if r < rounds - 1:
            pl.semaphore_signal(sib_free, inc=1, device_id=sibling, device_id_type=MESH)

    def rows_of(way, sub, t):
        sign = 1 - 2 * way
        index = lax.rem(place - sign * t + 2 * chips, chips)
        return pl.ds(pl.multiple_of(index * piece + sub * part, 16), part)

    def ring(r, way, sub, t, target):
        return pltpu.make_async_remote_copy(
            src_ref=acc(r, way, rows_of(way, sub, t)),
            dst_ref=target,
            send_sem=ring_send.at[r, way, sub, lax.rem(t, 2)],
            recv_sem=ring_recv.at[r, way, sub, t],
            device_id=ways[way],
            device_id_type=MESH,
        )

    def adding(r, way, sub, t):
        return ring(r, way, sub, t, slots.at[r, way, rows_of(way, sub, t)])

    def handing(r, way, sub, t):
        return ring(r, way, sub, t, acc(r, way, rows_of(way, sub, t)))

    def share(r, way, rs):
        return pltpu.make_async_remote_copy(
            src_ref=acc(r, way, rs),
            dst_ref=blocks_out.at[4 * r + 2 * core + way, rs],
            send_sem=share_send.at[r, way],
            recv_sem=share_recv.at[r, way],
            device_id=sibling,
            device_id_type=MESH,
        )

    def place_out(r, way, rs):
        block = blocks_out.at[4 * r + 2 * core + way, rs]
        return pltpu.make_async_copy(acc(r, way, rs), block, out_sem.at[r, way])

    def when(condition, way, t, body):
        if chips * piece > width:
            condition = condition & (rows_of(way, 0, t).start < width)
        if condition is True:
            body()
        elif condition is not False:
            pl.when(condition)(body)

    def chain(r, way, sub, t):
        def sent():
            adding(r, way, sub, t - 2).wait_send()

        def added():
            adding(r, way, sub, t - 1).wait_recv()
            rs = rows_of(way, sub, t)
            acc(r, way, rs)[...] = (
                acc(r, way, rs)[...].astype(f32) + slots[r, way, rs].astype(f32)
            ).astype(bf16)

        def kept():
            handing(r, way, sub, t - 1).wait_recv()

        def whole():
            share(r, way, rows_of(way, sub, t)).start()
            place_out(r, way, rows_of(way, sub, t)).start()

        when((t >= 2) & (t <= 2 * steps + 1), way, t - 2, sent)
        when((t >= 1) & (t <= steps), way, t, added)
        when((t >= 0) & (t < steps), way, t, lambda: adding(r, way, sub, t).start())
        when((t > steps) & (t <= 2 * steps), way, t, kept)
        when((t >= steps) & (t < 2 * steps), way, t, lambda: handing(r, way, sub, t).start())
        when((t >= steps) & (t <= 2 * steps), way, t, whole)

    def slot(tick, offsets):
        for r, offset in enumerate(offsets):
            for sub in range(subs):
                for way in (0, 1):
                    chain(r, way, sub, tick - offset)

    def back(i, block):
        return pltpu.make_async_remote_copy(
            src_ref=gsend.at[rows_at(block, half_rows)],
            dst_ref=gouter.at[half_at(i, block)],
            send_sem=back_send.at[block],
            recv_sem=back_recv.at[i, block],
            device_id=peer,
            device_id_type=MESH,
        )

    def grad_copy(i, block):
        source = gsum.at[rows_at(block, half_rows)]
        return pltpu.make_async_copy(source, grad_out.at[half_at(i, block)], grad_sem.at[block])

    early = (0, 3, 7)
    early_ticks = 8

    def backward_batch(turn, carry):
        i = MB - 1 - turn
        mine = rows_at(i, rows)

        def need(what):
            if what == "unit_ffn":

                @pl.when((turn == 0) & (rank == 1))
                def _():
                    g_load().wait()

                @pl.when(turn > 0)
                def _():
                    unspill(1).wait()
                    for block in (0, 1):
                        grad_copy(MB - 1, block).wait()

            if what == "hidden":

                @pl.when(turn > 0)
                def _():
                    unspill(0).start()

            if what == "middle":

                @pl.when(turn == 0)
                def _():
                    for k in range(MB):
                        acts_copy(k).wait()

                        @pl.when(rank == 0)
                        def _():
                            for block in (0, 1):
                                forth(k, block).wait_send()

                @pl.when(turn > 0)
                def _():
                    unspill(0).wait()

            if what == "attention":

                @pl.when(turn == 0)
                def _():
                    unspill(1).start()

        def hook(what, k):
            now = (turn == MB - 1) & (rank == 0)

            def at(condition, tick, rounds_now):
                @pl.when(now & condition)
                def _():
                    slot(tick, early[:rounds_now])

            if what == "first":

                @pl.when(now)
                def _():
                    compute(0)
                    slot(0, early[:1])

            if what == "hidden":
                at(k == 3, 1, 1)
            if what == "hidden_end":

                @pl.when(now)
                def _():
                    compute(1, lambda: slot(2, early[:1]))
                    slot(3, early[:2])

            if what == "middle":
                at(k == 1, 4, 2)
            if what == "attention" and k == 3:
                at(True, 5, 2)
            if what == "attention_end":

                @pl.when(now)
                def _():
                    compute(2, lambda: slot(6, early[:2]))
                    slot(7, early)

        def grad_of(block):
            @pl.when(rank == 0)
            def _():
                back(i, block).wait_recv()

            return gouter[half_at(i, block), :].astype(f32)

        def unit_of(block):
            rs = rows_at(block, half_rows)
            return jnp.where(turn == 0, gsum[rs, :], unit[rs, :])

        def give(block, value):
            @pl.when((turn > 0) & (rank == 1))
            def _():
                back(MB - 1, block).wait_send()

            rs = rows_at(block, half_rows)
            rounded = value.astype(bf16)
            gsend[rs, :] = rounded
            gsum[rs, :] = jnp.where(rank == 1, rounded.astype(f32), value)
            grad_copy(i, block).start()

            @pl.when(rank == 1)
            def _():
                back(i, block).start()

        backward_block(
            grad_of,
            unit_of,
            weights,
            vec,
            need,
            lengths[i],
            [ref.at[mine] for ref in (qkv, mixed, stats, slope)],
            (unit, gouter.at[mine], gatt.at[mine], gmix, gsum),
            sums,
            give,
            hook,
        )
        return carry

    lax.fori_loop(0, MB, backward_batch, 0)

    def sum_step(bit):
        return pltpu.make_async_remote_copy(
            src_ref=totals,
            dst_ref=total_slots.at[bit],
            send_sem=sum_send.at[bit],
            recv_sem=sum_recv.at[bit],
            device_id=across(bit),
            device_id_type=MESH,
        )

    @pl.when(rank == 1)
    def _():
        compute(0)

    start = jnp.where(rank == 0, early_ticks, 0)
    offsets = [jnp.where(rank == 0, early[r], r) for r in range(rounds)]

    def rest(tick, carry):
        slot(tick, offsets)
        for r in range(1, rounds):

            @pl.when((rank == 1) & (tick == r - 1))
            def _():
                compute(r)

        for bit in range(bits + 1):

            @pl.when(tick - start == 2 + bit)
            def _():
                if bit > 0:
                    sum_step(bit - 1).wait()
                    totals[...] += total_slots[bit - 1]
                if bit < bits:
                    sum_step(bit).start()

        return carry

    lax.fori_loop(start, offsets[-1] + 2 * steps + 2, rest, 0)
    sum_copy = pltpu.make_async_copy(totals, sums_out, sum_out_sem)
    sum_copy.start()
    for block in (0, 1):
        grad_copy(0, block).wait()

        @pl.when(rank == 1)
        def _():
            back(0, block).wait_send()

    everything = pl.ds(0, width)
    for r in range(rounds):
        for way in (0, 1):
            share(r, way, everything).wait_recv()
            share(r, way, everything).wait_send()
            place_out(r, way, everything).wait()
    sum_copy.wait()


def finish_kernel(acts, grads, blocks, sums, *refs):
    acts_out, grads_out, refs = refs[0], refs[1], refs[2:]
    outs, vectors, refs = refs[:4], refs[4 : 4 + len(SUM_ROWS) + 1], refs[5 + len(SUM_ROWS) :]
    taken, wide, acts_kept, grads_kept, in_sem, out_sem, copy_sem = refs
    depth, width = taken.shape[0], sums.shape[1]
    ways = ((acts, acts_kept, acts_out), (grads, grads_kept, grads_out))
    copies_in = [
        pltpu.make_async_copy(source, kept, copy_sem.at[k])
        for k, (source, kept, _) in enumerate(ways)
    ]
    copies_out = [
        pltpu.make_async_copy(kept, out.at[0], copy_sem.at[k])
        for k, (_, kept, out) in enumerate(ways)
    ]

    def target(k):
        if k < 4:
            return outs[0].at[0, pl.ds(k * width, width)]
        if k < 8:
            return outs[1].at[0, :, pl.ds((k - 4) * width, width)]
        if k < 9:
            return outs[2].at[0]
        return outs[3].at[0, :, pl.ds((k - 9) * width, width)]

    def load(k):
        return pltpu.make_async_copy(blocks.at[k], taken.at[k % depth], in_sem.at[k % depth])

    def store(k):
        return pltpu.make_async_copy(wide.at[k % depth], target(k), out_sem.at[k % depth])

    count = blocks.shape[0]
    for k in range(depth):
        load(k).start()
    for copy in copies_in:
        copy.start()
    for k, out in enumerate(vectors[:-1]):
        out[...] = sums[k : k + 1, :]
    for j in range(vectors[-1].shape[1] // width):
        row = len(SUM_ROWS) + j
        vectors[-1][:, j * width : (j + 1) * width] = sums[row : row + 1, :]
    for k in range(count):
        load(k).wait()
        if k >= depth:
            store(k - depth).wait()
        wide[k % depth] = taken[k % depth].astype(f32)
        store(k).start()
        if k + depth < count:
            load(k + depth).start()
        elif k + depth == count:
            for copy_in, copy_out in zip(copies_in, copies_out):
                copy_in.wait()
                copy_out.start()
    for k in range(count - depth, count):
        store(k).wait()
    for copy in copies_out:
        copy.wait()


def per_device(chips, *args):
    x_input = args[0]
    names = (
        "w_qkv", "bias_query", "bias_value", "w_out", "bias_out", "gain_attn", "shift_attn",
        "w_in", "bias_in", "w_back", "bias_back", "gain_ffn", "shift_ffn",
    )
    given = dict(zip(names, args[1:14]))
    lengths, cotangent = args[14:]
    row_count, width = x_input.shape
    rows = row_count // MB
    hidden = given["w_in"].shape[2]
    weights = [given[name] for name in ("w_qkv", "w_out", "w_in", "w_back")]
    anywhere = pl.BlockSpec(memory_space=pl.ANY)
    vmem = pl.BlockSpec(memory_space=pltpu.VMEM)
    smem = pl.BlockSpec(memory_space=pltpu.SMEM)
    dma = pltpu.SemaphoreType.DMA
    shape = jax.ShapeDtypeStruct
    weight_scratch = [pltpu.VMEM(w.shape[1:], bf16) for w in weights]
    kept = [
        (width, bf16),
        (3 * width, bf16),
        (width, bf16),
        (LANES, f32),
        (hidden, bf16),
        (hidden, bf16),
        (width, bf16),
    ]
    rounds = (3 * width + width + 2 * hidden) // (4 * width)
    subs = 2 if width % (32 * chips) == 0 else 1
    steps = chips - 1
    bits = (2 * chips).bit_length() - 1
    square = (width, width)

    def whole_rows(columns):
        return [pltpu.VMEM((row_count, n), kind) for n, kind in columns]

    acts, input_grads, blocks, totals, _ = pl.pallas_call(
        functools.partial(layer_kernel, chips),
        out_shape=[
            shape((row_count, width), bf16),
            shape((row_count, width), f32),
            shape((4 * rounds, *square), bf16),
            shape((SUM_COUNT, width), f32),
            shape((2, rows, width), f32),
        ],
        in_specs=[anywhere] * 6 + [vmem] * len(FORWARD_VECTORS) + [smem],
        out_specs=[anywhere] * 5,
        scratch_shapes=weight_scratch
        + whole_rows(kept)
        + whole_rows([(width, bf16)] * 2)
        + [
            pltpu.VMEM((rows, width), bf16),
            pltpu.VMEM((rows, width), bf16),
            pltpu.VMEM((rows, width), f32),
            pltpu.VMEM((rows, width), f32),
            pltpu.VMEM((SUM_COUNT, width), f32),
            pltpu.VMEM((bits, SUM_COUNT, width), f32),
            pltpu.VMEM((2, *square), bf16),
            pltpu.VMEM((rounds, 2, *square), bf16),
            dma((5,)),
            dma((MB,)),
            dma,
            dma((2,)),
            dma((MB,)),
            dma((MB, 2)),
            dma((MB, 2)),
            dma((2,)),
            dma((MB, 2)),
            dma((2,)),
            dma((2,)),
            dma((2,)),
            pltpu.SemaphoreType.REGULAR,
            dma((rounds, 2, subs, 2)),
            dma((rounds, 2, subs, 2 * steps)),
            dma((rounds, 2)),
            dma((rounds, 2)),
            dma((bits,)),
            dma((bits,)),
            dma((rounds, 2)),
            dma,
        ],
        compiler_params=pltpu.CompilerParams(
            collective_id=0, has_side_effects=True, vmem_limit_bytes=VMEM_LIMIT
        ),
        name="layer",
    )(x_input, cotangent, *weights, *[given[name] for name in FORWARD_VECTORS], lengths)
    vector_names = SUM_ROWS + ("bias_in",)
    depth = 4
    acts, input_grads, *whole = pl.pallas_call(
        finish_kernel,
        out_shape=[
            shape((1, row_count, width), bf16),
            shape((1, row_count, width), f32),
            shape((1, hidden, width), f32),
            shape((1, width, hidden), f32),
            shape((1, width, width), f32),
            shape((1, width, 3 * width), f32),
        ]
        + [shape(given[name].shape, f32) for name in vector_names],
        in_specs=[anywhere] * 3 + [vmem],
        out_specs=[anywhere] * 6 + [vmem] * len(vector_names),
        scratch_shapes=[
            pltpu.VMEM((depth, *square), bf16),
            pltpu.VMEM((depth, *square), f32),
            pltpu.VMEM((row_count, width), bf16),
            pltpu.VMEM((row_count, width), f32),
            dma((depth,)),
            dma((depth,)),
            dma((2,)),
        ],
        compiler_params=pltpu.CompilerParams(vmem_limit_bytes=VMEM_LIMIT),
        name="finish",
    )(acts, input_grads, blocks, totals)
    grads = dict(zip(("w_back", "w_in", "w_out", "w_qkv") + vector_names, whole))
    return (acts, input_grads, *[grads[name] for name in names])


def solution(mesh):
    return jax.shard_map(
        functools.partial(per_device, mesh.shape["dp"] // 2),
        mesh=mesh,
        in_specs=(
            P("dp", None),
            P("section", None, None),
            P("section", None),
            P("section", None),
            P("section", None, None),
            P("section", None),
            P("section", None),
            P("section", None),
            P("section", None, None),
            P("section", None),
            P("section", None, None),
            P("section", None),
            P("section", None),
            P("section", None),
            P("dp"),
            P("dp", None),
        ),
        out_specs=(
            P("section", "dp", None),
            P("section", "dp", None),
            P("section", None, None),
            P("section", None),
            P("section", None),
            P("section", None, None),
            P("section", None),
            P("section", None),
            P("section", None),
            P("section", None, None),
            P("section", None),
            P("section", None, None),
            P("section", None),
            P("section", None),
            P("section", None),
        ),
        check_vma=False,
    )
```

```python
import functools

import jax
import jax.numpy as jnp
from jax import lax
from jax.experimental import pallas as pl
from jax.experimental.pallas import tpu as pltpu
from jax.sharding import PartitionSpec as P

HEAD = 64
LANES = 128
MB = 2
EPSILON = 1e-12
DEAD = -1e30
FACTOR_ATTN = 12
FACTOR_FFN = 13
STAT_COLUMNS = 16
TURN_PAIRS = 2
FORWARD_PAIRS = 3
VMEM_LIMIT = 62 << 20

FORWARD_VECTORS = (
    "bias_query",
    "bias_value",
    "bias_out",
    "gain_attn",
    "shift_attn",
    "bias_in",
    "bias_back",
    "gain_ffn",
    "shift_ffn",
)
SUM_ROWS = tuple(name for name in FORWARD_VECTORS if name != "bias_in")
SUM_COUNT = 16

f32 = jnp.float32
bf16 = jnp.bfloat16
MESH = pl.DeviceIdType.MESH
NN = (((1,), (0,)), ((), ()))
NT = (((1,), (1,)), ((), ()))
TN = (((0,), (0,)), ((), ()))


def mm(left, right, dims=NN):
    return lax.dot_general(left, right, dims, preferred_element_type=f32)


def only_if(condition):
    if isinstance(condition, bool):
        return (lambda body: body()) if condition else (lambda body: None)
    return pl.when(condition)


def rows_at(index, count):
    return pl.ds(pl.multiple_of(index * count, count), count)


def norm_rows(value):
    centred = value - jnp.mean(value, axis=-1, keepdims=True)
    factor = lax.rsqrt(jnp.mean(centred * centred, axis=-1, keepdims=True) + EPSILON)
    return centred * factor, factor


def norm_back(grad_hat, unit, factor):
    return factor * (
        grad_hat
        - jnp.mean(grad_hat, axis=-1, keepdims=True)
        - unit * jnp.mean(grad_hat * unit, axis=-1, keepdims=True)
    )


def column_sum(value):
    return jnp.sum(value, axis=0, keepdims=True)


def split_three(value):
    high = value.astype(bf16)
    rest = value - high.astype(f32)
    middle = rest.astype(bf16)
    low = (rest - middle.astype(f32)).astype(bf16)
    return high, middle, low


def key_bias(rows, length):
    key = lax.broadcasted_iota(jnp.int32, (rows, LANES), 0)
    return jnp.where(key < length, 0.0, DEAD).astype(bf16)


def attention_forward(qkv, mixed, stats, logs, length, width):
    rows = qkv.shape[0]
    lane = lax.broadcasted_iota(jnp.int32, (rows, LANES), 1)
    dead = key_bias(rows, length)
    zero = jnp.zeros((rows, LANES), bf16)
    one = jnp.ones((rows, LANES), bf16)

    def turn_of(turn, carry):
        def columns(part, head):
            at = part * width + (turn * FORWARD_PAIRS + head // 2) * LANES
            return pl.ds(pl.multiple_of(at, LANES), LANES)

        def marked(part, head, mark):
            own = (lane < HEAD) if head % 2 == 0 else (lane >= HEAD)
            mark = jnp.where(lane == HEAD - HEAD * (head % 2), mark, zero)
            return jnp.where(own, qkv[:, columns(part, head)], mark)

        def scores_of(head):
            return mm(marked(1, head, dead), marked(0, head, one), NT)

        heads = 2 * FORWARD_PAIRS
        ahead = [scores_of(0), scores_of(1)]
        outs = []
        for head in range(heads):
            if head + 2 < heads:
                ahead.append(scores_of(head + 2))
            scores = ahead[head]
            ahead[head] = None
            highest = jnp.max(scores, axis=0, keepdims=True)
            weights = jnp.exp(scores - highest).astype(bf16)
            product = mm(marked(2, head, one).T, weights)
            odd = head % 2
            total = product[HEAD - HEAD * odd : HEAD - HEAD * odd + 1]
            outs.append(product[HEAD * odd : HEAD * odd + HEAD] * (1.0 / total))
            logs[pl.ds(turn * heads + head, 1), :] = highest + jnp.log(total)
            if odd:
                mixed[:, columns(0, head)] = jnp.concatenate(outs, 0).T.astype(bf16)
                outs = []
        return carry

    lax.fori_loop(0, width // (FORWARD_PAIRS * LANES), turn_of, 0)
    stats[:, :STAT_COLUMNS] = logs[...].T


def forward_block(weights, vec, need, length, saved, logs, unit1, unit2, result, send, done):
    w_qkv, w_out, w_in, w_back = weights
    x, qkv, mixed, stats, slope, active, normed = saved
    rows, width = x.shape
    half_rows = rows // 2
    scale = HEAD ** -0.5
    need("query")
    qkv[:, :width] = ((mm(x[...], w_qkv[:, :width]) + vec["bias_query"][...]) * scale).astype(bf16)
    need("key")
    qkv[:, width : 2 * width] = mm(x[...], w_qkv[:, width : 2 * width]).astype(bf16)
    qkv[:, 2 * width :] = (mm(x[...], w_qkv[:, 2 * width :]) + vec["bias_value"][...]).astype(bf16)
    attention_forward(qkv, mixed, stats, logs, length, width)
    lane = lax.broadcasted_iota(jnp.int32, (half_rows, LANES), 1)
    need("out")

    def after_attention(block, carry):
        rs = rows_at(block, half_rows)
        summed = x[rs, :].astype(f32) + mm(mixed[rs, :], w_out[...]) + vec["bias_out"][...]
        unit, factor = norm_rows(summed)
        unit1[rs, :] = unit
        normed[rs, :] = (unit * vec["gain_attn"][...] + vec["shift_attn"][...]).astype(bf16)
        stats[rs, :] = jnp.where(lane == FACTOR_ATTN, factor, stats[rs, :])
        return carry

    lax.fori_loop(0, 2, after_attention, 0)
    done("attn")
    need("in")

    def hidden(j, carry):
        cs = rows_at(j, width)
        inner = mm(normed[...], w_in[:, cs]) + vec["bias_in"][:, cs]
        share = 0.5 * (1.0 + lax.erf(inner * 0.7071067811865476))
        active[:, cs] = (inner * share).astype(bf16)
        slope[:, cs] = (
            share + inner * jnp.exp(-0.5 * inner * inner) * 0.3989422804014327
        ).astype(bf16)
        return carry

    lax.fori_loop(0, w_in.shape[1] // width, hidden, 0)
    need("back")

    def after_ffn(block, carry):
        rs = rows_at(block, half_rows)
        summed = normed[rs, :].astype(f32) + mm(active[rs, :], w_back[...]) + vec["bias_back"][...]
        unit, factor = norm_rows(summed)
        unit2[rs, :] = unit
        result[rs, :] = (unit * vec["gain_ffn"][...] + vec["shift_ffn"][...]).astype(bf16)
        stats[rs, :] = jnp.where(lane == FACTOR_FFN, factor, stats[rs, :])
        send(block)
        return carry

    lax.fori_loop(0, 2, after_ffn, 0)
    done("ffn")


def attention_backward(qkv, gmix, mixed, stats, length, width, sums, between):
    rows = qkv.shape[0]
    lane = lax.broadcasted_iota(jnp.int32, (rows, LANES), 1)
    dead = key_bias(rows, length)
    zero = jnp.zeros((rows, LANES), bf16)
    one = jnp.ones((rows, LANES), bf16)

    def turn_of(turn, carry):
        heads = 2 * TURN_PAIRS

        def columns(part, head):
            at = part * width + (turn * TURN_PAIRS + head // 2) * LANES
            return pl.ds(pl.multiple_of(at, LANES), LANES)

        def operands(head):
            q2, k2, v2 = [qkv[:, columns(part, head)] for part in range(3)]
            g2, mixed2 = gmix[:, columns(0, head)], mixed[:, columns(0, head)]
            own = (lane < HEAD) if head % 2 == 0 else (lane >= HEAD)
            at = HEAD - HEAD * (head % 2)
            terms = jnp.where(own, g2.astype(f32) * mixed2.astype(f32), 0.0)
            logs = jnp.where(lane == turn * heads + head, stats[...], 0.0)
            d0, d1, d2 = split_three(-jnp.sum(terms, axis=-1, keepdims=True))
            l0, l1, l2 = split_three(-jnp.sum(logs, axis=-1, keepdims=True))
            m0, m1, m2, m3 = [lane == at + t for t in range(4)]
            m012 = m0 | m1 | m2
            qa = jnp.where(
                own,
                q2,
                jnp.where(m0, l0, jnp.where(m1, l1, jnp.where(m2, l2, jnp.where(m3, one, zero)))),
            )
            ga = jnp.where(own, g2, jnp.where(m0, d0, jnp.where(m1, d1, jnp.where(m2, d2, zero))))
            ka = jnp.where(own, k2, jnp.where(m012, one, jnp.where(m3, dead, zero)))
            va = jnp.where(own, v2, jnp.where(m012, one, zero))
            first = HEAD * (head % 2)
            return q2, g2, k2.T[first : first + HEAD], mm(ka, qa, NT), mm(va, ga, NT)

        ahead = operands(0)
        grads = []
        for head in range(heads):
            q2, g2, k2_t, scores, grad_probs = ahead
            if head + 1 < heads:
                ahead = operands(head + 1)
            probs = jnp.exp(scores)
            grad_scores = (probs * grad_probs).astype(bf16)
            grads.append((mm(k2_t, grad_scores), mm(grad_scores, q2), mm(probs.astype(bf16), g2)))
            if head % 2:
                even, odd = grads
                grads = []
                grad_q = jnp.concatenate([even[0], odd[0]], 0).T * (HEAD ** -0.5)
                grad_k = jnp.where(lane < HEAD, even[1], odd[1])
                grad_v = jnp.where(lane < HEAD, even[2], odd[2])
                for part, grad in enumerate((grad_q, grad_k, grad_v)):
                    qkv[:, columns(part, head)] = grad.astype(bf16)
                cols = columns(0, head)
                sums["bias_query"][:, cols] += column_sum(grad_q)
                sums["bias_value"][:, cols] += column_sum(grad_v)
        between(turn)
        return carry

    lax.fori_loop(0, width // (TURN_PAIRS * LANES), turn_of, 0)


def backward_block(grad_of, unit_of, weights, vec, need, length, saved, work, sums, give, hook):
    w_qkv, w_out, w_in, w_back = weights
    qkv, mixed, stats, slope = saved
    unit, gouter, gatt, gmix, gsum = work
    rows, width = gsum.shape
    half_rows = rows // 2
    need("unit_ffn")

    def first(block, carry):
        rs = rows_at(block, half_rows)
        grad, unit_rows = grad_of(block), unit_of(block)
        factor = stats[rs, FACTOR_FFN : FACTOR_FFN + 1]
        sums["gain_ffn"][...] += column_sum(grad * unit_rows)
        sums["shift_ffn"][...] += column_sum(grad)
        grad_sum = norm_back(grad * vec["gain_ffn"][...], unit_rows, factor)
        gsum[rs, :] = grad_sum
        gouter[rs, :] = grad_sum.astype(bf16)
        sums["bias_back"][...] += column_sum(grad_sum)
        return carry

    lax.fori_loop(0, 2, first, 0)
    hook("first", 0)
    need("hidden")

    def hidden(j, carry):
        cs = rows_at(j, width)
        grad_inner = mm(gouter[...], w_back[cs, :], NT) * slope[:, cs].astype(f32)
        sums["bias_in"](j)[...] += column_sum(grad_inner)
        slope[:, cs] = grad_inner.astype(bf16)
        hook("hidden", j)
        return carry

    lax.fori_loop(0, w_in.shape[1] // width, hidden, 0)
    hook("hidden_end", 0)
    need("middle")

    def middle(block, carry):
        rs = rows_at(block, half_rows)
        grad = gsum[rs, :] + mm(slope[rs, :], w_in[...], NT)
        unit_rows = unit[rs, :]
        factor = stats[rs, FACTOR_ATTN : FACTOR_ATTN + 1]
        sums["gain_attn"][...] += column_sum(grad * unit_rows)
        sums["shift_attn"][...] += column_sum(grad)
        grad_sum = norm_back(grad * vec["gain_attn"][...], unit_rows, factor)
        gsum[rs, :] = grad_sum
        rounded = grad_sum.astype(bf16)
        gatt[rs, :] = rounded
        sums["bias_out"][...] += column_sum(grad_sum)
        gmix[rs, :] = mm(rounded, w_out[...], NT).astype(bf16)
        hook("middle", block)
        return carry

    lax.fori_loop(0, 2, middle, 0)
    hook("middle_end", 0)
    need("attention")
    attention_backward(
        qkv, gmix, mixed, stats, length, width, sums, lambda h: hook("attention", h)
    )
    hook("attention_end", 0)
    need("last")

    def last(block, carry):
        rs = rows_at(block, half_rows)
        give(block, gsum[rs, :] + mm(qkv[rs, :], w_qkv[...], NT))
        hook("last", block)
        return carry

    lax.fori_loop(0, 2, last, 0)


def layer_kernel(chips, *refs):
    (x_in, cotangent, w_qkv, w_out, w_in, w_back), refs = refs[:6], refs[6:]
    vec, refs = dict(zip(FORWARD_VECTORS, refs)), refs[len(FORWARD_VECTORS) :]
    lengths, refs = refs[0], refs[1:]
    acts_out, grad_out, blocks_out, sums_out, units_out, refs = *refs[:5], refs[5:]
    weights, refs = refs[:4], refs[4:]
    mixed_x, attended_qkv, stats, slope, active, normed, refs = *refs[:6], refs[6:]
    gouter, gmix, gsend, gsum, unit, totals, total_slots, refs = *refs[:7], refs[7:]
    logs, acc_first, slots, refs = *refs[:3], refs[3:]
    weight_sem, x_sem, g_sem, unit_sem, acts_sem, forth_send, forth_recv, refs = *refs[:7], refs[7:]
    back_send, back_recv, grad_sem, sib_send, sib_recv, sib_free, refs = *refs[:6], refs[6:]
    ring_send, ring_recv, share_send, share_recv, sum_send, sum_recv, refs = *refs[:6], refs[6:]
    out_sem, sum_out_sem = refs
    rank = lax.axis_index("section")
    me = lax.axis_index("dp")
    peer = (1 - rank, me)
    rows, width = gsum.shape
    half_rows = rows // 2
    mixed, x_kept = [mixed_x.at[:, pl.ds(k * width, width)] for k in range(2)]
    gatt = attended_qkv.at[:, pl.ds(0, width)]
    qkv = attended_qkv.at[:, pl.ds(width, 3 * width)]

    core = lax.rem(me, 2)
    chip = lax.div(me, 2)
    ring_half = chips // 2
    place = jnp.where(lax.rem(chip, 2) == 0, lax.div(chip, 2), chips - 1 - lax.div(chip, 2))
    rounds, _, subs = ring_recv.shape[:3]
    piece = -(-width // (16 * subs * chips)) * 16 * subs
    part = piece // subs
    steps = chips - 1
    bits = total_slots.shape[0]

    def device_at(position):
        position = lax.rem(position + chips, chips)
        spot = jnp.where(position < ring_half, 2 * position, 2 * (chips - 1 - position) + 1)
        return (rank, 2 * spot + core)

    sibling = (rank, me + 1 - 2 * core)
    ways = (device_at(place + 1), device_at(place - 1))

    def across(bit):
        size = 1 << bit
        return (rank, me + size - 2 * size * lax.rem(lax.div(me, size), 2))

    def half_at(i, block):
        return pl.ds(pl.multiple_of(i * rows + block * half_rows, half_rows), half_rows)

    query = pl.ds(0, width)
    key_value = pl.ds(width, 2 * width)
    loads = dict(
        query=(w_qkv.at[0, :, query], weights[0].at[:, query]),
        key=(w_qkv.at[0, :, key_value], weights[0].at[:, key_value]),
        out=(w_out.at[0], weights[1]),
        back=(w_back.at[0], weights[3]),
    )
    loads["in"] = (w_in.at[0], weights[2])
    order = ("query", "key", "out", "in", "back")
    loads = {
        name: pltpu.make_async_copy(*loads[name], weight_sem.at[k]) for k, name in enumerate(order)
    }

    def x_load(i):
        rs = rows_at(i, rows)
        return pltpu.make_async_copy(x_in.at[rs], x_kept.at[rs], x_sem.at[i])

    def g_load():
        return pltpu.make_async_copy(cotangent, gouter, g_sem)

    @pl.when(rank == 0)
    def _():
        x_load(0).start()

    loads["query"].start()
    loads["key"].start()
    barrier = pltpu.get_barrier_semaphore()
    partners = [peer, sibling, *ways] + [across(bit) for bit in range(1, bits)]
    for partner in partners:
        pl.semaphore_signal(barrier, inc=1, device_id=partner, device_id_type=MESH)
    totals[...] = jnp.zeros_like(totals)
    sums = {name: totals.at[pl.ds(k, 1)] for k, name in enumerate(SUM_ROWS)}
    sums["bias_in"] = lambda j: totals.at[pl.ds(len(SUM_ROWS) + j, 1)]
    pl.semaphore_wait(barrier, len(partners))

    def forth(i, block):
        rs = half_at(i, block)
        return pltpu.make_async_remote_copy(
            src_ref=gatt.at[rs],
            dst_ref=x_kept.at[rs],
            send_sem=forth_send.at[i, block],
            recv_sem=forth_recv.at[i, block],
            device_id=peer,
            device_id_type=MESH,
        )

    def acts_copy(i):
        rs = rows_at(i, rows)
        return pltpu.make_async_copy(gatt.at[rs], acts_out.at[rs], acts_sem.at[i])

    def spill(k):
        return pltpu.make_async_copy((unit, gsum)[k], units_out.at[k], unit_sem.at[k])

    def unspill(k):
        return pltpu.make_async_copy(units_out.at[k], unit, unit_sem.at[k])

    def forward_batch(i, carry):
        mine = rows_at(i, rows)

        @pl.when(rank == 0)
        def _():
            x_load(i).wait()

        @pl.when(rank == 1)
        def _():
            forth(i, 0).wait_recv()
            forth(i, 1).wait_recv()

        def need(what):
            @pl.when(i == 0)
            def _():
                loads[what].wait()
                if what == "key":
                    loads["out"].start()
                    loads["in"].start()
                if what == "out":
                    loads["back"].start()

                    @pl.when(rank == 0)
                    def _():
                        x_load(1).start()

                    @pl.when(rank == 1)
                    def _():
                        g_load().start()

            if what in ("out", "back"):

                @pl.when(i > 0)
                def _():
                    spill(0 if what == "out" else 1).wait()

        def done(what):
            @pl.when(i < MB - 1)
            def _():
                spill(0 if what == "attn" else 1).start()

            if what == "ffn":
                acts_copy(i).start()

        def send(block):
            @pl.when(rank == 0)
            def _():
                forth(i, block).start()

        forward_block(
            weights,
            vec,
            need,
            lengths[i],
            [ref.at[mine] for ref in (x_kept, qkv, mixed, stats, slope, active, normed)],
            logs,
            unit,
            gsum,
            gatt.at[mine],
            send,
            done,
        )
        return carry

    lax.fori_loop(0, MB, forward_batch, 0)

    def acc(r, way, rs=None):
        rs = pl.ds(0, width) if rs is None else rs
        if r == 0:
            return acc_first.at[way, rs]
        return weights[3].at[pl.ds(pl.multiple_of((2 * r - 2 + way) * width + rs.start, 16), rs.size)]

    def sibling_term(r, way):
        if r == 0:
            return slots.at[1, way]
        return active.at[pl.ds(0, width), rows_at(way, width)]

    def to_sibling(r, way):
        return pltpu.make_async_remote_copy(
            src_ref=acc(r, way),
            dst_ref=sibling_term(r, way),
            send_sem=sib_send.at[way],
            recv_sem=sib_recv.at[way],
            device_id=sibling,
            device_id_type=MESH,
        )

    def compute_into(r, owner, way, tile):
        j = 2 * owner + way
        here = pl.ds(pl.multiple_of(tile * tile_rows, tile_rows), tile_rows)
        there = acc(r, way, here)

        left, at, right = (
            (active, j * width, gouter),
            (normed, 0, slope.at[:, rows_at(j, width)]),
            (mixed_x, jnp.minimum(j, 1) * width, attended_qkv.at[:, rows_at(j, width)]),
        )[r]
        cs = pl.ds(pl.multiple_of(at + tile * tile_rows, LANES), tile_rows)
        there[...] = mm(left[:, cs], right[...], TN).astype(bf16)

    tiles = 2
    tile_rows = width // tiles
    add_rows = 64

    def compute(r, between=lambda: None):
        if r > 0:
            pl.semaphore_wait(sib_free, 1)

        def for_sibling(step, carry):
            way, tile = lax.div(step, tiles), lax.rem(step, tiles)
            compute_into(r, 1 - core, way, tile)

            @pl.when(tile == tiles - 1)
            def _():
                to_sibling(r, way).start()

            return carry

        lax.fori_loop(0, 2 * tiles, for_sibling, 0)
        between()

        def for_me(step, carry):
            way, tile = lax.div(step, tiles), lax.rem(step, tiles)

            @pl.when(tile == 0)
            def _():
                to_sibling(r, way).wait_send()

            compute_into(r, core, way, tile)
            return carry

        lax.fori_loop(0, 2 * tiles, for_me, 0)
        for way in (0, 1):
            to_sibling(r, way).wait_recv()

            def add(k, carry):
                rs = rows_at(k, add_rows)
                mine, other = acc(r, way, rs), sibling_term(r, way).at[rs]
                mine[...] = (mine[...].astype(f32) + other[...].astype(f32)).astype(bf16)
                return carry

            lax.fori_loop(0, width // add_rows, add, 0)
        if r < rounds - 1:
            pl.semaphore_signal(sib_free, inc=1, device_id=sibling, device_id_type=MESH)

    def rows_of(way, sub, t):
        sign = 1 - 2 * way
        index = lax.rem(place - sign * t + 2 * chips, chips)
        return pl.ds(pl.multiple_of(index * piece + sub * part, 16), part)

    def ring(r, way, sub, t, target):
        return pltpu.make_async_remote_copy(
            src_ref=acc(r, way, rows_of(way, sub, t)),
            dst_ref=target,
            send_sem=ring_send.at[r, way, sub, lax.rem(t, 2)],
            recv_sem=ring_recv.at[r, way, sub, t],
            device_id=ways[way],
            device_id_type=MESH,
        )

    def adding(r, way, sub, t):
        return ring(r, way, sub, t, slots.at[r, way, rows_of(way, sub, t)])

    def handing(r, way, sub, t):
        return ring(r, way, sub, t, acc(r, way, rows_of(way, sub, t)))

    def share(r, way, rs):
        return pltpu.make_async_remote_copy(
            src_ref=acc(r, way, rs),
            dst_ref=blocks_out.at[4 * r + 2 * core + way, rs],
            send_sem=share_send.at[r, way],
            recv_sem=share_recv.at[r, way],
            device_id=sibling,
            device_id_type=MESH,
        )

    def place_out(r, way, rs):
        block = blocks_out.at[4 * r + 2 * core + way, rs]
        return pltpu.make_async_copy(acc(r, way, rs), block, out_sem.at[r, way])

    def when(condition, way, t, body):
        if chips * piece > width:
            condition = condition & (rows_of(way, 0, t).start < width)
        if condition is True:
            body()
        elif condition is not False:
            pl.when(condition)(body)

    def chain(r, way, sub, t):
        def sent():
            adding(r, way, sub, t - 2).wait_send()

        def added():
            adding(r, way, sub, t - 1).wait_recv()
            rs = rows_of(way, sub, t)
            acc(r, way, rs)[...] = (
                acc(r, way, rs)[...].astype(f32) + slots[r, way, rs].astype(f32)
            ).astype(bf16)

        def kept():
            handing(r, way, sub, t - 1).wait_recv()

        def whole():
            share(r, way, rows_of(way, sub, t)).start()
            place_out(r, way, rows_of(way, sub, t)).start()

        when((t >= 2) & (t <= 2 * steps + 1), way, t - 2, sent)
        when((t >= 1) & (t <= steps), way, t, added)
        when((t >= 0) & (t < steps), way, t, lambda: adding(r, way, sub, t).start())
        when((t > steps) & (t <= 2 * steps), way, t, kept)
        when((t >= steps) & (t < 2 * steps), way, t, lambda: handing(r, way, sub, t).start())
        when((t >= steps) & (t <= 2 * steps), way, t, whole)

    def slot(tick, offsets):
        for r, offset in enumerate(offsets):
            for sub in range(subs):
                for way in (0, 1):
                    chain(r, way, sub, tick - offset)

    def back(i, block):
        return pltpu.make_async_remote_copy(
            src_ref=gsend.at[rows_at(block, half_rows)],
            dst_ref=gouter.at[half_at(i, block)],
            send_sem=back_send.at[block],
            recv_sem=back_recv.at[i, block],
            device_id=peer,
            device_id_type=MESH,
        )

    def grad_copy(i, block):
        source = gsum.at[rows_at(block, half_rows)]
        return pltpu.make_async_copy(source, grad_out.at[half_at(i, block)], grad_sem.at[block])

    early = (0, 3, 9)
    early_ticks = 12

    def backward_batch(turn, rank, hooked):
        i = MB - 1 - turn
        mine = rows_at(i, rows)

        def need(what):
            if what == "unit_ffn":

                @only_if((turn == 0) & (rank == 1))
                def _():
                    g_load().wait()

                @only_if(turn > 0)
                def _():
                    unspill(1).wait()
                    for block in (0, 1):
                        grad_copy(MB - 1, block).wait()

            if what == "hidden":

                @only_if(turn > 0)
                def _():
                    unspill(0).start()

            if what == "middle":

                @only_if(turn == 0)
                def _():
                    for k in range(MB):
                        acts_copy(k).wait()

                        @only_if(rank == 0)
                        def _():
                            for block in (0, 1):
                                forth(k, block).wait_send()

                @only_if(turn > 0)
                def _():
                    unspill(0).wait()

            if what == "attention":

                @only_if(turn == 0)
                def _():
                    unspill(1).start()

        def hook(what, k):
            if not hooked:
                return

            def at(condition, tick, rounds_now):
                @only_if(condition)
                def _():
                    slot(tick, early[:rounds_now])

            if what == "first":
                compute(0)
                slot(0, early[:1])

            if what == "hidden":
                at(k == 3, 1, 1)
            if what == "hidden_end":
                compute(1, lambda: slot(2, early[:1]))
                slot(3, early[:2])

            if what == "middle":
                at(k == 1, 4, 2)
            if what == "attention":
                slot(5 + k, early[:2])
            if what == "attention_end":
                compute(2, lambda: slot(8, early[:2]))
                slot(9, early)

            if what == "last":
                at(k == 0, 10, 3)
                at(k == 0, 11, 3)

        def grad_of(block):
            @only_if(rank == 0)
            def _():
                back(i, block).wait_recv()

            return gouter[half_at(i, block), :].astype(f32)

        def unit_of(block):
            rs = rows_at(block, half_rows)
            if isinstance(turn, int):
                return (gsum if turn == 0 else unit)[rs, :]
            return jnp.where(turn == 0, gsum[rs, :], unit[rs, :])

        def give(block, value):
            @only_if((turn > 0) & (rank == 1))
            def _():
                back(MB - 1, block).wait_send()

            rs = rows_at(block, half_rows)
            rounded = value.astype(bf16)
            gsend[rs, :] = rounded
            if hooked:
                gsum[rs, :] = value
            else:
                gsum[rs, :] = jnp.where(rank == 1, rounded.astype(f32), value)
            grad_copy(i, block).start()

            @only_if(rank == 1)
            def _():
                back(i, block).start()

        backward_block(
            grad_of,
            unit_of,
            weights,
            vec,
            need,
            lengths[i],
            [ref.at[mine] for ref in (qkv, mixed, stats, slope)],
            (unit, gouter.at[mine], gatt.at[mine], gmix, gsum),
            sums,
            give,
            hook,
        )

    def plain(turn, carry):
        backward_batch(turn, rank, False)
        return carry

    lax.fori_loop(0, jnp.where(rank == 0, MB - 1, MB), plain, 0)

    @pl.when(rank == 0)
    def _():
        backward_batch(MB - 1, 0, True)


    def sum_step(bit):
        return pltpu.make_async_remote_copy(
            src_ref=totals,
            dst_ref=total_slots.at[bit],
            send_sem=sum_send.at[bit],
            recv_sem=sum_recv.at[bit],
            device_id=across(bit),
            device_id_type=MESH,
        )

    late = (0, 1, 2)

    @pl.when(rank == 1)
    def _():
        compute(0)
        slot(0, late[:1])
        compute(1)
        slot(1, late[:2])
        compute(2)

    start = jnp.where(rank == 0, early_ticks, 2)
    offsets = [jnp.where(rank == 0, early[r], late[r]) for r in range(rounds)]

    def rest(tick, carry):
        slot(tick, offsets)
        for bit in range(bits + 1):

            @pl.when(tick - start == 2 + bit)
            def _():
                if bit > 0:
                    sum_step(bit - 1).wait()
                    totals[...] += total_slots[bit - 1]
                if bit < bits:
                    sum_step(bit).start()

        return carry

    lax.fori_loop(start, offsets[-1] + 2 * steps + 2, rest, 0)
    sum_copy = pltpu.make_async_copy(totals, sums_out, sum_out_sem)
    sum_copy.start()
    for block in (0, 1):
        grad_copy(0, block).wait()

        @pl.when(rank == 1)
        def _():
            back(0, block).wait_send()

    everything = pl.ds(0, width)
    for r in range(rounds):
        for way in (0, 1):
            share(r, way, everything).wait_recv()
            share(r, way, everything).wait_send()
            place_out(r, way, everything).wait()
    sum_copy.wait()


def finish_kernel(acts, grads, blocks, sums, *refs):
    acts_out, grads_out, refs = refs[0], refs[1], refs[2:]
    outs, vectors, refs = refs[:4], refs[4 : 4 + len(SUM_ROWS) + 1], refs[5 + len(SUM_ROWS) :]
    taken, wide, acts_kept, grads_kept, in_sem, out_sem, copy_sem = refs
    depth, width = taken.shape[0], sums.shape[1]
    ways = ((acts, acts_kept, acts_out), (grads, grads_kept, grads_out))
    copies_in = [
        pltpu.make_async_copy(source, kept, copy_sem.at[k])
        for k, (source, kept, _) in enumerate(ways)
    ]
    copies_out = [
        pltpu.make_async_copy(kept, out.at[0], copy_sem.at[k])
        for k, (_, kept, out) in enumerate(ways)
    ]

    def target(k):
        if k < 4:
            return outs[0].at[0, pl.ds(k * width, width)]
        if k < 8:
            return outs[1].at[0, :, pl.ds((k - 4) * width, width)]
        if k < 9:
            return outs[2].at[0]
        return outs[3].at[0, :, pl.ds((k - 9) * width, width)]

    def load(k):
        return pltpu.make_async_copy(blocks.at[k], taken.at[k % depth], in_sem.at[k % depth])

    def store(k):
        return pltpu.make_async_copy(wide.at[k % depth], target(k), out_sem.at[k % depth])

    count = blocks.shape[0]
    for k in range(depth):
        load(k).start()
    for copy in copies_in:
        copy.start()
    for k, out in enumerate(vectors[:-1]):
        out[...] = sums[k : k + 1, :]
    for j in range(vectors[-1].shape[1] // width):
        row = len(SUM_ROWS) + j
        vectors[-1][:, j * width : (j + 1) * width] = sums[row : row + 1, :]
    for k in range(count):
        load(k).wait()
        if k >= depth:
            store(k - depth).wait()
        wide[k % depth] = taken[k % depth].astype(f32)
        store(k).start()
        if k + depth < count:
            load(k + depth).start()
        elif k + depth == count:
            for copy_in, copy_out in zip(copies_in, copies_out):
                copy_in.wait()
                copy_out.start()
    for k in range(count - depth, count):
        store(k).wait()
    for copy in copies_out:
        copy.wait()


def per_device(chips, *args):
    x_input = args[0]
    names = (
        "w_qkv", "bias_query", "bias_value", "w_out", "bias_out", "gain_attn", "shift_attn",
        "w_in", "bias_in", "w_back", "bias_back", "gain_ffn", "shift_ffn",
    )
    given = dict(zip(names, args[1:14]))
    lengths, cotangent = args[14:]
    row_count, width = x_input.shape
    rows = row_count // MB
    hidden = given["w_in"].shape[2]
    weights = [given[name] for name in ("w_qkv", "w_out", "w_in", "w_back")]
    anywhere = pl.BlockSpec(memory_space=pl.ANY)
    vmem = pl.BlockSpec(memory_space=pltpu.VMEM)
    smem = pl.BlockSpec(memory_space=pltpu.SMEM)
    dma = pltpu.SemaphoreType.DMA
    shape = jax.ShapeDtypeStruct
    weight_scratch = [pltpu.VMEM(w.shape[1:], bf16) for w in weights]
    kept = [
        (2 * width, bf16),
        (4 * width, bf16),
        (LANES, f32),
        (hidden, bf16),
        (hidden, bf16),
        (width, bf16),
    ]
    rounds = (3 * width + width + 2 * hidden) // (4 * width)
    subs = 2 if width % (32 * chips) == 0 else 1
    steps = chips - 1
    bits = (2 * chips).bit_length() - 1
    square = (width, width)

    def whole_rows(columns):
        return [pltpu.VMEM((row_count, n), kind) for n, kind in columns]

    acts, input_grads, blocks, totals, _ = pl.pallas_call(
        functools.partial(layer_kernel, chips),
        out_shape=[
            shape((row_count, width), bf16),
            shape((row_count, width), f32),
            shape((4 * rounds, *square), bf16),
            shape((SUM_COUNT, width), f32),
            shape((2, rows, width), f32),
        ],
        in_specs=[anywhere] * 6 + [vmem] * len(FORWARD_VECTORS) + [smem],
        out_specs=[anywhere] * 5,
        scratch_shapes=weight_scratch
        + whole_rows(kept)
        + whole_rows([(width, bf16)])
        + [
            pltpu.VMEM((rows, width), bf16),
            pltpu.VMEM((rows, width), bf16),
            pltpu.VMEM((rows, width), f32),
            pltpu.VMEM((rows, width), f32),
            pltpu.VMEM((SUM_COUNT, width), f32),
            pltpu.VMEM((bits, SUM_COUNT, width), f32),
            pltpu.VMEM((STAT_COLUMNS, rows), f32),
            pltpu.VMEM((2, *square), bf16),
            pltpu.VMEM((rounds, 2, *square), bf16),
            dma((5,)),
            dma((MB,)),
            dma,
            dma((2,)),
            dma((MB,)),
            dma((MB, 2)),
            dma((MB, 2)),
            dma((2,)),
            dma((MB, 2)),
            dma((2,)),
            dma((2,)),
            dma((2,)),
            pltpu.SemaphoreType.REGULAR,
            dma((rounds, 2, subs, 2)),
            dma((rounds, 2, subs, 2 * steps)),
            dma((rounds, 2)),
            dma((rounds, 2)),
            dma((bits,)),
            dma((bits,)),
            dma((rounds, 2)),
            dma,
        ],
        compiler_params=pltpu.CompilerParams(
            collective_id=0, has_side_effects=True, vmem_limit_bytes=VMEM_LIMIT
        ),
        name="layer",
    )(x_input, cotangent, *weights, *[given[name] for name in FORWARD_VECTORS], lengths)
    vector_names = SUM_ROWS + ("bias_in",)
    depth = 4
    acts, input_grads, *whole = pl.pallas_call(
        finish_kernel,
        out_shape=[
            shape((1, row_count, width), bf16),
            shape((1, row_count, width), f32),
            shape((1, hidden, width), f32),
            shape((1, width, hidden), f32),
            shape((1, width, width), f32),
            shape((1, width, 3 * width), f32),
        ]
        + [shape(given[name].shape, f32) for name in vector_names],
        in_specs=[anywhere] * 3 + [vmem],
        out_specs=[anywhere] * 6 + [vmem] * len(vector_names),
        scratch_shapes=[
            pltpu.VMEM((depth, *square), bf16),
            pltpu.VMEM((depth, *square), f32),
            pltpu.VMEM((row_count, width), bf16),
            pltpu.VMEM((row_count, width), f32),
            dma((depth,)),
            dma((depth,)),
            dma((2,)),
        ],
        compiler_params=pltpu.CompilerParams(vmem_limit_bytes=VMEM_LIMIT),
        name="finish",
    )(acts, input_grads, blocks, totals)
    grads = dict(zip(("w_back", "w_in", "w_out", "w_qkv") + vector_names, whole))
    return (acts, input_grads, *[grads[name] for name in names])


def solution(mesh):
    return jax.shard_map(
        functools.partial(per_device, mesh.shape["dp"] // 2),
        mesh=mesh,
        in_specs=(
            P("dp", None),
            P("section", None, None),
            P("section", None),
            P("section", None),
            P("section", None, None),
            P("section", None),
            P("section", None),
            P("section", None),
            P("section", None, None),
            P("section", None),
            P("section", None, None),
            P("section", None),
            P("section", None),
            P("section", None),
            P("dp"),
            P("dp", None),
        ),
        out_specs=(
            P("section", "dp", None),
            P("section", "dp", None),
            P("section", None, None),
            P("section", None),
            P("section", None),
            P("section", None, None),
            P("section", None),
            P("section", None),
            P("section", None),
            P("section", None, None),
            P("section", None),
            P("section", None, None),
            P("section", None),
            P("section", None),
            P("section", None),
        ),
        check_vma=False,
    )
```

```python
import functools

import jax
import jax.numpy as jnp
from jax import lax
from jax.experimental import pallas as pl
from jax.experimental.pallas import tpu as pltpu
from jax.sharding import PartitionSpec as P

HEAD = 64
LANES = 128
MB = 2
EPSILON = 1e-12
DEAD = -1e30
FACTOR_ATTN = 12
FACTOR_FFN = 13
STAT_COLUMNS = 16
TURN_PAIRS = 6
FORWARD_PAIRS = 6
VMEM_LIMIT = 62 << 20

FORWARD_VECTORS = (
    "bias_query",
    "bias_value",
    "bias_out",
    "gain_attn",
    "shift_attn",
    "bias_in",
    "bias_back",
    "gain_ffn",
    "shift_ffn",
)
SUM_ROWS = tuple(name for name in FORWARD_VECTORS if name != "bias_in")
SUM_COUNT = 16

f32 = jnp.float32
bf16 = jnp.bfloat16
MESH = pl.DeviceIdType.MESH
NN = (((1,), (0,)), ((), ()))
NT = (((1,), (1,)), ((), ()))
TN = (((0,), (0,)), ((), ()))


def mm(left, right, dims=NN):
    return lax.dot_general(left, right, dims, preferred_element_type=f32)


def only_if(condition):
    if isinstance(condition, bool):
        return (lambda body: body()) if condition else (lambda body: None)
    return pl.when(condition)


def rows_at(index, count):
    return pl.ds(pl.multiple_of(index * count, count), count)


def norm_rows(value):
    centred = value - jnp.mean(value, axis=-1, keepdims=True)
    factor = lax.rsqrt(jnp.mean(centred * centred, axis=-1, keepdims=True) + EPSILON)
    return centred * factor, factor


def norm_back(grad_hat, unit, factor):
    return factor * (
        grad_hat
        - jnp.mean(grad_hat, axis=-1, keepdims=True)
        - unit * jnp.mean(grad_hat * unit, axis=-1, keepdims=True)
    )


def column_sum(value):
    return jnp.sum(value, axis=0, keepdims=True)


def split_three(value):
    high = value.astype(bf16)
    rest = value - high.astype(f32)
    middle = rest.astype(bf16)
    low = (rest - middle.astype(f32)).astype(bf16)
    return high, middle, low


def key_bias(rows, length):
    key = lax.broadcasted_iota(jnp.int32, (rows, LANES), 0)
    return jnp.where(key < length, 0.0, DEAD).astype(bf16)


def attention_forward(qkv, mixed, stats, logs, length, width):
    rows = qkv.shape[0]
    lane = lax.broadcasted_iota(jnp.int32, (rows, LANES), 1)
    dead = key_bias(rows, length)
    zero = jnp.zeros((rows, LANES), bf16)
    one = jnp.ones((rows, LANES), bf16)

    def turn_of(turn, carry):
        def columns(part, head):
            at = part * width + (turn * FORWARD_PAIRS + head // 2) * LANES
            return pl.ds(pl.multiple_of(at, LANES), LANES)

        def marked(part, head, mark):
            own = (lane < HEAD) if head % 2 == 0 else (lane >= HEAD)
            mark = jnp.where(lane == HEAD - HEAD * (head % 2), mark, zero)
            return jnp.where(own, qkv[:, columns(part, head)], mark)

        def scores_of(head):
            return mm(marked(1, head, dead), marked(0, head, one), NT)

        heads = 2 * FORWARD_PAIRS
        ahead = [scores_of(0), scores_of(1)]
        outs = []
        for head in range(heads):
            if head + 2 < heads:
                ahead.append(scores_of(head + 2))
            scores = ahead[head]
            ahead[head] = None
            highest = jnp.max(scores, axis=0, keepdims=True)
            weights = jnp.exp(scores - highest).astype(bf16)
            product = mm(marked(2, head, one).T, weights)
            odd = head % 2
            total = product[HEAD - HEAD * odd : HEAD - HEAD * odd + 1]
            outs.append(product[HEAD * odd : HEAD * odd + HEAD] * (1.0 / total))
            logs[pl.ds(turn * heads + head, 1), :] = highest + jnp.log(total)
            if odd:
                mixed[:, columns(0, head)] = jnp.concatenate(outs, 0).T.astype(bf16)
                outs = []
        return carry

    turns = width // (FORWARD_PAIRS * LANES)
    if turns == 1:
        turn_of(0, 0)
    else:
        lax.fori_loop(0, turns, turn_of, 0)
    stats[:, :STAT_COLUMNS] = logs[...].T


def forward_block(weights, vec, need, length, saved, logs, unit1, unit2, result, send, done):
    w_qkv, w_out, w_in, w_back = weights
    x, qkv, mixed, stats, slope, active, normed = saved
    rows, width = x.shape
    half_rows = rows // 2
    scale = HEAD ** -0.5
    need("query")
    qkv[:, :width] = ((mm(x[...], w_qkv[:, :width]) + vec["bias_query"][...]) * scale).astype(bf16)
    need("key")
    qkv[:, width : 2 * width] = mm(x[...], w_qkv[:, width : 2 * width]).astype(bf16)
    qkv[:, 2 * width :] = (mm(x[...], w_qkv[:, 2 * width :]) + vec["bias_value"][...]).astype(bf16)
    attention_forward(qkv, mixed, stats, logs, length, width)
    lane = lax.broadcasted_iota(jnp.int32, (half_rows, LANES), 1)
    need("out")

    def after_attention(block, carry):
        rs = rows_at(block, half_rows)
        summed = x[rs, :].astype(f32) + mm(mixed[rs, :], w_out[...]) + vec["bias_out"][...]
        unit, factor = norm_rows(summed)
        unit1[rs, :] = unit
        normed[rs, :] = (unit * vec["gain_attn"][...] + vec["shift_attn"][...]).astype(bf16)
        stats[rs, :] = jnp.where(lane == FACTOR_ATTN, factor, stats[rs, :])
        return carry

    lax.fori_loop(0, 2, after_attention, 0)
    done("attn")
    need("in")
    need("back")

    def ffn(block, carry):
        rs = rows_at(block, half_rows)

        def hidden(j, carry):
            cs = rows_at(j, width)
            inner = mm(normed[rs, :], w_in[:, cs]) + vec["bias_in"][:, cs]
            share = 0.5 * (1.0 + lax.erf(inner * 0.7071067811865476))
            active[rs, cs] = (inner * share).astype(bf16)
            slope[rs, cs] = (
                share + inner * jnp.exp(-0.5 * inner * inner) * 0.3989422804014327
            ).astype(bf16)
            return carry

        lax.fori_loop(0, w_in.shape[1] // width, hidden, 0)
        summed = normed[rs, :].astype(f32) + mm(active[rs, :], w_back[...]) + vec["bias_back"][...]
        unit, factor = norm_rows(summed)
        unit2[rs, :] = unit
        result[rs, :] = (unit * vec["gain_ffn"][...] + vec["shift_ffn"][...]).astype(bf16)
        stats[rs, :] = jnp.where(lane == FACTOR_FFN, factor, stats[rs, :])
        send(block)
        return carry

    lax.fori_loop(0, 2, ffn, 0)
    done("ffn")


def attention_backward(qkv, gmix, mixed, stats, length, width, sums, between):
    rows = qkv.shape[0]
    lane = lax.broadcasted_iota(jnp.int32, (rows, LANES), 1)
    dead = key_bias(rows, length)
    zero = jnp.zeros((rows, LANES), bf16)
    one = jnp.ones((rows, LANES), bf16)

    def turn_of(turn, carry):
        heads = 2 * TURN_PAIRS

        def columns(part, head):
            at = part * width + (turn * TURN_PAIRS + head // 2) * LANES
            return pl.ds(pl.multiple_of(at, LANES), LANES)

        def log_total(head):
            if isinstance(turn, int):
                return stats[:, turn * heads + head : turn * heads + head + 1]
            logs = jnp.where(lane == turn * heads + head, stats[...], 0.0)
            return jnp.sum(logs, axis=-1, keepdims=True)

        def operands(head):
            q2, k2, v2 = [qkv[:, columns(part, head)] for part in range(3)]
            g2, mixed2 = gmix[:, columns(0, head)], mixed[:, columns(0, head)]
            own = (lane < HEAD) if head % 2 == 0 else (lane >= HEAD)
            at = HEAD - HEAD * (head % 2)
            terms = jnp.where(own, g2.astype(f32) * mixed2.astype(f32), 0.0)
            d0, d1, d2 = split_three(-jnp.sum(terms, axis=-1, keepdims=True))
            l0, l1, l2 = split_three(-log_total(head))
            m0, m1, m2, m3 = [lane == at + t for t in range(4)]
            m012 = m0 | m1 | m2
            qa = jnp.where(
                own,
                q2,
                jnp.where(m0, l0, jnp.where(m1, l1, jnp.where(m2, l2, jnp.where(m3, one, zero)))),
            )
            ga = jnp.where(own, g2, jnp.where(m0, d0, jnp.where(m1, d1, jnp.where(m2, d2, zero))))
            ka = jnp.where(own, k2, jnp.where(m012, one, jnp.where(m3, dead, zero)))
            va = jnp.where(own, v2, jnp.where(m012, one, zero))
            first = HEAD * (head % 2)
            return q2, g2, k2.T[first : first + HEAD], mm(ka, qa, NT), mm(va, ga, NT)

        ahead = operands(0)
        grads = []
        for head in range(heads):
            q2, g2, k2_t, scores, grad_probs = ahead
            if head + 1 < heads:
                ahead = operands(head + 1)
            probs = jnp.exp(scores)
            grad_scores = (probs * grad_probs).astype(bf16)
            grads.append((mm(k2_t, grad_scores), mm(grad_scores, q2), mm(probs.astype(bf16), g2)))
            if head % 2:
                even, odd = grads
                grads = []
                grad_q = jnp.concatenate([even[0], odd[0]], 0).T * (HEAD ** -0.5)
                grad_k = jnp.where(lane < HEAD, even[1], odd[1])
                grad_v = jnp.where(lane < HEAD, even[2], odd[2])
                for part, grad in enumerate((grad_q, grad_k, grad_v)):
                    qkv[:, columns(part, head)] = grad.astype(bf16)
                cols = columns(0, head)
                sums["bias_query"][:, cols] += column_sum(grad_q)
                sums["bias_value"][:, cols] += column_sum(grad_v)
                between(turn * TURN_PAIRS + head // 2)
        return carry

    turns = width // (TURN_PAIRS * LANES)
    if turns == 1:
        turn_of(0, 0)
    else:
        lax.fori_loop(0, turns, turn_of, 0)


def backward_block(grad_of, unit_of, weights, vec, need, length, saved, work, sums, give, hook):
    w_qkv, w_out, w_in, w_back = weights
    qkv, mixed, stats, slope = saved
    unit, gouter, gatt, gmix, gsum = work
    rows, width = gsum.shape
    half_rows = rows // 2
    need("unit_ffn")

    def first(block, carry):
        rs = rows_at(block, half_rows)
        grad, unit_rows = grad_of(block), unit_of(block)
        factor = stats[rs, FACTOR_FFN : FACTOR_FFN + 1]
        sums["gain_ffn"][...] += column_sum(grad * unit_rows)
        sums["shift_ffn"][...] += column_sum(grad)
        grad_sum = norm_back(grad * vec["gain_ffn"][...], unit_rows, factor)
        gsum[rs, :] = grad_sum
        gouter[rs, :] = grad_sum.astype(bf16)
        sums["bias_back"][...] += column_sum(grad_sum)
        return carry

    lax.fori_loop(0, 2, first, 0)
    hook("first", 0)
    need("hidden")

    def hidden(j, carry):
        cs = rows_at(j, width)
        grad_inner = mm(gouter[...], w_back[cs, :], NT) * slope[:, cs].astype(f32)
        sums["bias_in"](j)[...] += column_sum(grad_inner)
        slope[:, cs] = grad_inner.astype(bf16)
        hook("hidden", j)
        return carry

    lax.fori_loop(0, w_in.shape[1] // width, hidden, 0)
    hook("hidden_end", 0)
    need("middle")

    def middle(block, carry):
        rs = rows_at(block, half_rows)
        grad = gsum[rs, :] + mm(slope[rs, :], w_in[...], NT)
        unit_rows = unit[rs, :]
        factor = stats[rs, FACTOR_ATTN : FACTOR_ATTN + 1]
        sums["gain_attn"][...] += column_sum(grad * unit_rows)
        sums["shift_attn"][...] += column_sum(grad)
        grad_sum = norm_back(grad * vec["gain_attn"][...], unit_rows, factor)
        gsum[rs, :] = grad_sum
        rounded = grad_sum.astype(bf16)
        gatt[rs, :] = rounded
        sums["bias_out"][...] += column_sum(grad_sum)
        gmix[rs, :] = mm(rounded, w_out[...], NT).astype(bf16)
        hook("middle", block)
        return carry

    lax.fori_loop(0, 2, middle, 0)
    hook("middle_end", 0)
    need("attention")
    attention_backward(
        qkv, gmix, mixed, stats, length, width, sums, lambda h: hook("attention", h)
    )
    hook("attention_end", 0)
    need("last")

    def last(block, carry):
        rs = rows_at(block, half_rows)
        give(block, gsum[rs, :] + mm(qkv[rs, :], w_qkv[...], NT))
        hook("last", block)
        return carry

    lax.fori_loop(0, 2, last, 0)


def layer_kernel(chips, *refs):
    (x_in, cotangent, w_qkv, w_out, w_in, w_back), refs = refs[:6], refs[6:]
    vec, refs = dict(zip(FORWARD_VECTORS, refs)), refs[len(FORWARD_VECTORS) :]
    lengths, refs = refs[0], refs[1:]
    acts_out, grad_out, blocks_out, sums_out, units_out, refs = *refs[:5], refs[5:]
    weights, refs = refs[:4], refs[4:]
    mixed_x, attended_qkv, stats, slope, active, normed, refs = *refs[:6], refs[6:]
    gouter, gmix, gsend, gsum, unit, totals, total_slots, refs = *refs[:7], refs[7:]
    logs, acc_first, slots, refs = *refs[:3], refs[3:]
    weight_sem, x_sem, g_sem, unit_sem, acts_sem, forth_send, forth_recv, refs = *refs[:7], refs[7:]
    back_send, back_recv, grad_sem, sib_send, sib_recv, sib_free, refs = *refs[:6], refs[6:]
    ring_send, ring_recv, share_send, share_recv, sum_send, sum_recv, refs = *refs[:6], refs[6:]
    out_sem, sum_out_sem = refs
    rank = lax.axis_index("section")
    me = lax.axis_index("dp")
    peer = (1 - rank, me)
    rows, width = gsum.shape
    half_rows = rows // 2
    mixed, x_kept = [mixed_x.at[:, pl.ds(k * width, width)] for k in range(2)]
    gatt = attended_qkv.at[:, pl.ds(0, width)]
    qkv = attended_qkv.at[:, pl.ds(width, 3 * width)]

    core = lax.rem(me, 2)
    chip = lax.div(me, 2)
    ring_half = chips // 2
    place = jnp.where(lax.rem(chip, 2) == 0, lax.div(chip, 2), chips - 1 - lax.div(chip, 2))
    rounds, _, subs = ring_recv.shape[:3]
    piece = -(-width // (16 * subs * chips)) * 16 * subs
    part = piece // subs
    steps = chips - 1
    bits = total_slots.shape[0]

    def device_at(position):
        position = lax.rem(position + chips, chips)
        spot = jnp.where(position < ring_half, 2 * position, 2 * (chips - 1 - position) + 1)
        return (rank, 2 * spot + core)

    sibling = (rank, me + 1 - 2 * core)
    def way_to(way):
        return device_at(place + 1 - 2 * way)

    def across(bit):
        size = 1 << bit
        return (rank, me + size - 2 * size * lax.rem(lax.div(me, size), 2))

    def half_at(i, block):
        return pl.ds(pl.multiple_of(i * rows + block * half_rows, half_rows), half_rows)

    query = pl.ds(0, width)
    key_value = pl.ds(width, 2 * width)
    loads = dict(
        query=(w_qkv.at[0, :, query], weights[0].at[:, query]),
        key=(w_qkv.at[0, :, key_value], weights[0].at[:, key_value]),
        out=(w_out.at[0], weights[1]),
        back=(w_back.at[0], weights[3]),
    )
    loads["in"] = (w_in.at[0], weights[2])
    order = ("query", "key", "out", "in", "back")
    loads = {
        name: pltpu.make_async_copy(*loads[name], weight_sem.at[k]) for k, name in enumerate(order)
    }

    def x_load(i):
        rs = rows_at(i, rows)
        return pltpu.make_async_copy(x_in.at[rs], x_kept.at[rs], x_sem.at[i])

    def g_load():
        return pltpu.make_async_copy(cotangent, gouter, g_sem)

    @pl.when(rank == 0)
    def _():
        x_load(0).start()

    loads["query"].start()
    loads["key"].start()
    barrier = pltpu.get_barrier_semaphore()
    partners = [peer, sibling, way_to(0), way_to(1)] + [across(bit) for bit in range(1, bits)]
    for partner in partners:
        pl.semaphore_signal(barrier, inc=1, device_id=partner, device_id_type=MESH)
    totals[...] = jnp.zeros_like(totals)
    sums = {name: totals.at[pl.ds(k, 1)] for k, name in enumerate(SUM_ROWS)}
    sums["bias_in"] = lambda j: totals.at[pl.ds(len(SUM_ROWS) + j, 1)]
    pl.semaphore_wait(barrier, len(partners))

    def forth(i, block):
        rs = half_at(i, block)
        return pltpu.make_async_remote_copy(
            src_ref=gatt.at[rs],
            dst_ref=x_kept.at[rs],
            send_sem=forth_send.at[i, block],
            recv_sem=forth_recv.at[i, block],
            device_id=peer,
            device_id_type=MESH,
        )

    def acts_copy(i):
        rs = rows_at(i, rows)
        return pltpu.make_async_copy(gatt.at[rs], acts_out.at[rs], acts_sem.at[i])

    def spill(k):
        return pltpu.make_async_copy((unit, gsum)[k], units_out.at[k], unit_sem.at[k])

    def unspill(k):
        return pltpu.make_async_copy(units_out.at[k], unit, unit_sem.at[k])

    def forward_batch(i, carry):
        mine = rows_at(i, rows)

        @pl.when(rank == 0)
        def _():
            x_load(i).wait()

        @pl.when(rank == 1)
        def _():
            forth(i, 0).wait_recv()
            forth(i, 1).wait_recv()

        def need(what):
            @pl.when(i == 0)
            def _():
                loads[what].wait()
                if what == "key":
                    loads["out"].start()
                    loads["in"].start()
                    loads["back"].start()
                if what == "out":

                    @pl.when(rank == 0)
                    def _():
                        x_load(1).start()

                    @pl.when(rank == 1)
                    def _():
                        g_load().start()

            if what in ("out", "back"):

                @pl.when(i > 0)
                def _():
                    spill(0 if what == "out" else 1).wait()

        def done(what):
            @pl.when(i < MB - 1)
            def _():
                spill(0 if what == "attn" else 1).start()

            if what == "ffn":
                acts_copy(i).start()

        def send(block):
            @pl.when(rank == 0)
            def _():
                forth(i, block).start()

        forward_block(
            weights,
            vec,
            need,
            lengths[i],
            [ref.at[mine] for ref in (x_kept, qkv, mixed, stats, slope, active, normed)],
            logs,
            unit,
            gsum,
            gatt.at[mine],
            send,
            done,
        )
        return carry

    lax.fori_loop(0, MB, forward_batch, 0)

    def acc(r, way, rs=None):
        rs = pl.ds(0, width) if rs is None else rs
        if r == 0:
            return acc_first.at[way, rs]
        return weights[3].at[pl.ds(pl.multiple_of((2 * r - 2 + way) * width + rs.start, 16), rs.size)]

    def sibling_term(r, way):
        if r == 0:
            return slots.at[1, way]
        return active.at[pl.ds(0, width), rows_at(way, width)]

    tiles = 2
    tile_rows = width // tiles
    first_tile = jnp.minimum(lax.div(place * piece, tile_rows), tiles - 1)

    def to_sibling(r, way, tile):
        here = rows_at(tile, tile_rows)
        return pltpu.make_async_remote_copy(
            src_ref=acc(r, way, here),
            dst_ref=sibling_term(r, way).at[here],
            send_sem=sib_send.at[way, tile],
            recv_sem=sib_recv.at[way, tile],
            device_id=sibling,
            device_id_type=MESH,
        )

    def term(r, owner, way, tile):
        j = 2 * owner + way
        left, at, right = (
            (active, j * width, gouter),
            (normed, 0, slope.at[:, rows_at(j, width)]),
            (mixed_x, jnp.minimum(j, 1) * width, attended_qkv.at[:, rows_at(j, width)]),
        )[r]
        cs = pl.ds(pl.multiple_of(at + tile * tile_rows, LANES), tile_rows)
        return mm(left[:, cs], right[...], TN)

    def compute(r, between):
        if r > 0:
            pl.semaphore_wait(sib_free, 1)

        def one_tile(step, carry):
            tile = lax.rem(first_tile + step, tiles)
            here = rows_at(tile, tile_rows)

            def for_sibling(way, carry):
                acc(r, way, here)[...] = term(r, 1 - core, way, tile).astype(bf16)
                to_sibling(r, way, tile).start()
                return carry

            def for_me(way, carry):
                value = term(r, core, way, tile)
                to_sibling(r, way, tile).wait()
                other = sibling_term(r, way).at[here]
                acc(r, way, here)[...] = (value + other[...].astype(f32)).astype(bf16)
                return carry

            lax.fori_loop(0, 2, for_sibling, 0)
            lax.fori_loop(0, 2, for_me, 0)

            @pl.when(step == 0)
            def _():
                between()

            return carry

        lax.fori_loop(0, tiles, one_tile, 0)
        if r < rounds - 1:
            pl.semaphore_signal(sib_free, inc=1, device_id=sibling, device_id_type=MESH)

    def rows_of(way, sub, t):
        sign = 1 - 2 * way
        index = lax.rem(place - sign * t + 2 * chips, chips)
        return pl.ds(pl.multiple_of(index * piece + sub * part, 16), part)

    def ring(r, way, sub, t, target):
        return pltpu.make_async_remote_copy(
            src_ref=acc(r, way, rows_of(way, sub, t)),
            dst_ref=target,
            send_sem=ring_send.at[r, way, sub, lax.rem(t, 2)],
            recv_sem=ring_recv.at[r, way, sub, t],
            device_id=way_to(way),
            device_id_type=MESH,
        )

    def adding(r, way, sub, t):
        return ring(r, way, sub, t, slots.at[r, way, rows_of(way, sub, t)])

    def handing(r, way, sub, t):
        return ring(r, way, sub, t, acc(r, way, rows_of(way, sub, t)))

    def share(r, way, rs):
        return pltpu.make_async_remote_copy(
            src_ref=acc(r, way, rs),
            dst_ref=blocks_out.at[4 * r + 2 * core + way, rs],
            send_sem=share_send.at[r, way],
            recv_sem=share_recv.at[r, way],
            device_id=sibling,
            device_id_type=MESH,
        )

    def place_out(r, way, rs):
        block = blocks_out.at[4 * r + 2 * core + way, rs]
        return pltpu.make_async_copy(acc(r, way, rs), block, out_sem.at[r, way])

    def when(condition, way, t, body):
        if chips * piece > width:
            condition = condition & (rows_of(way, 0, t).start < width)
        if condition is True:
            body()
        elif condition is not False:
            pl.when(condition)(body)

    def chain(r, way, sub, t):
        def sent():
            adding(r, way, sub, t - 2).wait_send()

        def added():
            adding(r, way, sub, t - 1).wait_recv()
            rs = rows_of(way, sub, t)
            acc(r, way, rs)[...] = (
                acc(r, way, rs)[...].astype(f32) + slots[r, way, rs].astype(f32)
            ).astype(bf16)

        def kept():
            handing(r, way, sub, t - 1).wait_recv()

        def whole():
            share(r, way, rows_of(way, sub, t)).start()
            place_out(r, way, rows_of(way, sub, t)).start()

        when((t >= 2) & (t <= 2 * steps + 1), way, t - 2, sent)
        when((t >= 1) & (t <= steps), way, t, added)
        when((t >= 0) & (t < steps), way, t, lambda: adding(r, way, sub, t).start())
        when((t > steps) & (t <= 2 * steps), way, t, kept)
        when((t >= steps) & (t < 2 * steps), way, t, lambda: handing(r, way, sub, t).start())
        when((t >= steps) & (t <= 2 * steps), way, t, whole)

    def slot(tick, offsets):
        for r, offset in enumerate(offsets):

            def one_chain(k, carry):
                chain(r, lax.rem(k, 2), lax.div(k, 2), tick - offset)
                return carry

            lax.fori_loop(0, 2 * subs, one_chain, 0)

    def back(i, block):
        return pltpu.make_async_remote_copy(
            src_ref=gsend.at[rows_at(block, half_rows)],
            dst_ref=gouter.at[half_at(i, block)],
            send_sem=back_send.at[block],
            recv_sem=back_recv.at[i, block],
            device_id=peer,
            device_id_type=MESH,
        )

    def grad_copy(i, block):
        source = gsum.at[rows_at(block, half_rows)]
        return pltpu.make_async_copy(source, grad_out.at[half_at(i, block)], grad_sem.at[block])

    early = (0, 4, 11)
    early_ticks = 15

    def backward_batch(turn, rank, hooked):
        i = MB - 1 - turn
        mine = rows_at(i, rows)

        def need(what):
            if what == "unit_ffn":

                @only_if((turn == 0) & (rank == 1))
                def _():
                    g_load().wait()

                @only_if(turn > 0)
                def _():
                    unspill(1).wait()
                    for block in (0, 1):
                        grad_copy(MB - 1, block).wait()

            if what == "hidden":

                @only_if(turn > 0)
                def _():
                    unspill(0).start()

            if what == "middle":

                @only_if(turn == 0)
                def _():
                    for k in range(MB):
                        acts_copy(k).wait()

                        @only_if(rank == 0)
                        def _():
                            for block in (0, 1):
                                forth(k, block).wait_send()

                @only_if(turn > 0)
                def _():
                    unspill(0).wait()

            if what == "attention":

                @only_if(turn == 0)
                def _():
                    unspill(1).start()

        def hook(what, k):
            if what == "attention" and k % 2 == 0:
                return

            @only_if((turn == MB - 1) & (rank == 0))
            def _():
                ring_part(what, k)

        def ring_part(what, k):

            def at(condition, tick, rounds_now):
                @only_if(condition)
                def _():
                    slot(tick, early[:rounds_now])

            if what == "first":
                compute(0, lambda: slot(0, early[:1]))
                slot(1, early[:1])
            if what == "hidden":
                at(lax.rem(k, 2) == 1, 2 + lax.div(k, 2), 1)
            if what == "hidden_end":
                compute(1, lambda: slot(4, early[:2]))
                slot(5, early[:2])
            if what == "middle":
                slot(6 + k, early[:2])
            if what == "attention" and k % 2 == 1:
                slot(8 + k // 2, early[:2])
            if what == "attention_end":
                compute(2, lambda: slot(11, early))
                slot(12, early)
                slot(13, early)
            if what == "last":
                at(k == 1, 14, 3)

        def grad_of(block):
            @only_if(rank == 0)
            def _():
                back(i, block).wait_recv()

            return gouter[half_at(i, block), :].astype(f32)

        def unit_of(block):
            rs = rows_at(block, half_rows)
            if isinstance(turn, int):
                return (gsum if turn == 0 else unit)[rs, :]
            return jnp.where(turn == 0, gsum[rs, :], unit[rs, :])

        def give(block, value):
            @only_if((turn > 0) & (rank == 1))
            def _():
                back(MB - 1, block).wait_send()

            rs = rows_at(block, half_rows)
            rounded = value.astype(bf16)
            gsend[rs, :] = rounded
            if hooked:
                gsum[rs, :] = value
            else:
                gsum[rs, :] = jnp.where(rank == 1, rounded.astype(f32), value)
            grad_copy(i, block).start()

            @only_if(rank == 1)
            def _():
                back(i, block).start()

        backward_block(
            grad_of,
            unit_of,
            weights,
            vec,
            need,
            lengths[i],
            [ref.at[mine] for ref in (qkv, mixed, stats, slope)],
            (unit, gouter.at[mine], gatt.at[mine], gmix, gsum),
            sums,
            give,
            hook,
        )

    def plain(turn, carry):
        backward_batch(turn, rank, False)
        return carry

    lax.fori_loop(0, MB, plain, 0)


    def sum_step(bit):
        return pltpu.make_async_remote_copy(
            src_ref=totals,
            dst_ref=total_slots.at[bit],
            send_sem=sum_send.at[bit],
            recv_sem=sum_recv.at[bit],
            device_id=across(bit),
            device_id_type=MESH,
        )

    late = (0, 2, 4)
    late_ticks = 6

    @pl.when(rank == 1)
    def _():
        for r in range(rounds):
            compute(r, lambda: slot(2 * r, late[: r + 1]))
            slot(2 * r + 1, late[: r + 1])

    start = jnp.where(rank == 0, early_ticks, late_ticks)
    offsets = [jnp.where(rank == 0, early[r], late[r]) for r in range(rounds)]

    def rest(tick, carry):
        slot(tick, offsets)
        for bit in range(bits + 1):

            @pl.when(tick - start == 2 + bit)
            def _():
                if bit > 0:
                    sum_step(bit - 1).wait()
                    totals[...] += total_slots[bit - 1]
                if bit < bits:
                    sum_step(bit).start()

        return carry

    lax.fori_loop(start, offsets[-1] + 2 * steps + 2, rest, 0)
    sum_copy = pltpu.make_async_copy(totals, sums_out, sum_out_sem)
    sum_copy.start()
    for block in (0, 1):
        grad_copy(0, block).wait()

        @pl.when(rank == 1)
        def _():
            back(0, block).wait_send()

    everything = pl.ds(0, width)
    for r in range(rounds):
        for way in (0, 1):
            share(r, way, everything).wait_recv()
            share(r, way, everything).wait_send()
            place_out(r, way, everything).wait()
    sum_copy.wait()


def finish_kernel(acts, grads, blocks, sums, *refs):
    acts_out, grads_out, refs = refs[0], refs[1], refs[2:]
    outs, vectors, refs = refs[:4], refs[4 : 4 + len(SUM_ROWS) + 1], refs[5 + len(SUM_ROWS) :]
    taken, wide, acts_kept, grads_kept, in_sem, out_sem, copy_sem = refs
    depth, width = taken.shape[0], sums.shape[1]
    ways = ((acts, acts_kept, acts_out), (grads, grads_kept, grads_out))
    copies_in = [
        pltpu.make_async_copy(source, kept, copy_sem.at[k])
        for k, (source, kept, _) in enumerate(ways)
    ]
    copies_out = [
        pltpu.make_async_copy(kept, out.at[0], copy_sem.at[k])
        for k, (_, kept, out) in enumerate(ways)
    ]

    def target(k):
        if k < 4:
            return outs[0].at[0, pl.ds(k * width, width)]
        if k < 8:
            return outs[1].at[0, :, pl.ds((k - 4) * width, width)]
        if k < 9:
            return outs[2].at[0]
        return outs[3].at[0, :, pl.ds((k - 9) * width, width)]

    def load(k):
        return pltpu.make_async_copy(blocks.at[k], taken.at[k % depth], in_sem.at[k % depth])

    def store(k):
        return pltpu.make_async_copy(wide.at[k % depth], target(k), out_sem.at[k % depth])

    count = blocks.shape[0]
    for k in range(depth):
        load(k).start()
    for copy in copies_in:
        copy.start()
    for k, out in enumerate(vectors[:-1]):
        out[...] = sums[k : k + 1, :]
    for j in range(vectors[-1].shape[1] // width):
        row = len(SUM_ROWS) + j
        vectors[-1][:, j * width : (j + 1) * width] = sums[row : row + 1, :]
    for k in range(count):
        load(k).wait()
        if k >= depth:
            store(k - depth).wait()
        wide[k % depth] = taken[k % depth].astype(f32)
        store(k).start()
        if k + depth < count:
            load(k + depth).start()
        elif k + depth == count:
            for copy_in, copy_out in zip(copies_in, copies_out):
                copy_in.wait()
                copy_out.start()
    for k in range(count - depth, count):
        store(k).wait()
    for copy in copies_out:
        copy.wait()


def per_device(chips, *args):
    x_input = args[0]
    names = (
        "w_qkv", "bias_query", "bias_value", "w_out", "bias_out", "gain_attn", "shift_attn",
        "w_in", "bias_in", "w_back", "bias_back", "gain_ffn", "shift_ffn",
    )
    given = dict(zip(names, args[1:14]))
    lengths, cotangent = args[14:]
    row_count, width = x_input.shape
    rows = row_count // MB
    hidden = given["w_in"].shape[2]
    weights = [given[name] for name in ("w_qkv", "w_out", "w_in", "w_back")]
    anywhere = pl.BlockSpec(memory_space=pl.ANY)
    vmem = pl.BlockSpec(memory_space=pltpu.VMEM)
    smem = pl.BlockSpec(memory_space=pltpu.SMEM)
    dma = pltpu.SemaphoreType.DMA
    shape = jax.ShapeDtypeStruct
    weight_scratch = [pltpu.VMEM(w.shape[1:], bf16) for w in weights]
    kept = [
        (2 * width, bf16),
        (4 * width, bf16),
        (LANES, f32),
        (hidden, bf16),
        (hidden, bf16),
        (width, bf16),
    ]
    rounds = (3 * width + width + 2 * hidden) // (4 * width)
    subs = 2 if width % (32 * chips) == 0 else 1
    steps = chips - 1
    bits = (2 * chips).bit_length() - 1
    square = (width, width)

    def whole_rows(columns):
        return [pltpu.VMEM((row_count, n), kind) for n, kind in columns]

    acts, input_grads, blocks, totals, _ = pl.pallas_call(
        functools.partial(layer_kernel, chips),
        out_shape=[
            shape((row_count, width), bf16),
            shape((row_count, width), f32),
            shape((4 * rounds, *square), bf16),
            shape((SUM_COUNT, width), f32),
            shape((2, rows, width), f32),
        ],
        in_specs=[anywhere] * 6 + [vmem] * len(FORWARD_VECTORS) + [smem],
        out_specs=[anywhere] * 5,
        scratch_shapes=weight_scratch
        + whole_rows(kept)
        + whole_rows([(width, bf16)])
        + [
            pltpu.VMEM((rows, width), bf16),
            pltpu.VMEM((rows, width), bf16),
            pltpu.VMEM((rows, width), f32),
            pltpu.VMEM((rows, width), f32),
            pltpu.VMEM((SUM_COUNT, width), f32),
            pltpu.VMEM((bits, SUM_COUNT, width), f32),
            pltpu.VMEM((STAT_COLUMNS, rows), f32),
            pltpu.VMEM((2, *square), bf16),
            pltpu.VMEM((rounds, 2, *square), bf16),
            dma((5,)),
            dma((MB,)),
            dma,
            dma((2,)),
            dma((MB,)),
            dma((MB, 2)),
            dma((MB, 2)),
            dma((2,)),
            dma((MB, 2)),
            dma((2,)),
            dma((2, 2)),
            dma((2, 2)),
            pltpu.SemaphoreType.REGULAR,
            dma((rounds, 2, subs, 2)),
            dma((rounds, 2, subs, 2 * steps)),
            dma((rounds, 2)),
            dma((rounds, 2)),
            dma((bits,)),
            dma((bits,)),
            dma((rounds, 2)),
            dma,
        ],
        compiler_params=pltpu.CompilerParams(
            collective_id=0, has_side_effects=True, vmem_limit_bytes=VMEM_LIMIT
        ),
        name="layer",
    )(x_input, cotangent, *weights, *[given[name] for name in FORWARD_VECTORS], lengths)
    vector_names = SUM_ROWS + ("bias_in",)
    depth = 4
    acts, input_grads, *whole = pl.pallas_call(
        finish_kernel,
        out_shape=[
            shape((1, row_count, width), bf16),
            shape((1, row_count, width), f32),
            shape((1, hidden, width), f32),
            shape((1, width, hidden), f32),
            shape((1, width, width), f32),
            shape((1, width, 3 * width), f32),
        ]
        + [shape(given[name].shape, f32) for name in vector_names],
        in_specs=[anywhere] * 3 + [vmem],
        out_specs=[anywhere] * 6 + [vmem] * len(vector_names),
        scratch_shapes=[
            pltpu.VMEM((depth, *square), bf16),
            pltpu.VMEM((depth, *square), f32),
            pltpu.VMEM((row_count, width), bf16),
            pltpu.VMEM((row_count, width), f32),
            dma((depth,)),
            dma((depth,)),
            dma((2,)),
        ],
        compiler_params=pltpu.CompilerParams(vmem_limit_bytes=VMEM_LIMIT),
        name="finish",
    )(acts, input_grads, blocks, totals)
    grads = dict(zip(("w_back", "w_in", "w_out", "w_qkv") + vector_names, whole))
    return (acts, input_grads, *[grads[name] for name in names])


def solution(mesh):
    return jax.shard_map(
        functools.partial(per_device, mesh.shape["dp"] // 2),
        mesh=mesh,
        in_specs=(
            P("dp", None),
            P("section", None, None),
            P("section", None),
            P("section", None),
            P("section", None, None),
            P("section", None),
            P("section", None),
            P("section", None),
            P("section", None, None),
            P("section", None),
            P("section", None, None),
            P("section", None),
            P("section", None),
            P("section", None),
            P("dp"),
            P("dp", None),
        ),
        out_specs=(
            P("section", "dp", None),
            P("section", "dp", None),
            P("section", None, None),
            P("section", None),
            P("section", None),
            P("section", None, None),
            P("section", None),
            P("section", None),
            P("section", None),
            P("section", None, None),
            P("section", None),
            P("section", None, None),
            P("section", None),
            P("section", None),
            P("section", None),
        ),
        check_vma=False,
    )
```

```python
import functools

import jax
import jax.numpy as jnp
from jax import lax
from jax.experimental import pallas as pl
from jax.experimental.pallas import tpu as pltpu
from jax.sharding import PartitionSpec as P

HEAD = 64
LANES = 128
MB = 2
EPSILON = 1e-12
DEAD = -1e30
FACTOR_ATTN = 12
FACTOR_FFN = 13
STAT_COLUMNS = 16
TURN_PAIRS = 6
FORWARD_PAIRS = 6
VMEM_LIMIT = 62 << 20

FORWARD_VECTORS = (
    "bias_query",
    "bias_value",
    "bias_out",
    "gain_attn",
    "shift_attn",
    "bias_in",
    "bias_back",
    "gain_ffn",
    "shift_ffn",
)
SUM_ROWS = tuple(name for name in FORWARD_VECTORS if name != "bias_in")
SUM_COUNT = 16

f32 = jnp.float32
bf16 = jnp.bfloat16
MESH = pl.DeviceIdType.MESH
NN = (((1,), (0,)), ((), ()))
NT = (((1,), (1,)), ((), ()))
TN = (((0,), (0,)), ((), ()))


def mm(left, right, dims=NN):
    return lax.dot_general(left, right, dims, preferred_element_type=f32)


def only_if(condition):
    if isinstance(condition, bool):
        return (lambda body: body()) if condition else (lambda body: None)
    return pl.when(condition)


def rows_at(index, count):
    return pl.ds(pl.multiple_of(index * count, count), count)


def norm_rows(value):
    centred = value - jnp.mean(value, axis=-1, keepdims=True)
    factor = lax.rsqrt(jnp.mean(centred * centred, axis=-1, keepdims=True) + EPSILON)
    return centred * factor, factor


def norm_back(grad_hat, unit, factor):
    return factor * (
        grad_hat
        - jnp.mean(grad_hat, axis=-1, keepdims=True)
        - unit * jnp.mean(grad_hat * unit, axis=-1, keepdims=True)
    )


def column_sum(value):
    return jnp.sum(value, axis=0, keepdims=True)


def split_three(value):
    high = value.astype(bf16)
    rest = value - high.astype(f32)
    middle = rest.astype(bf16)
    low = (rest - middle.astype(f32)).astype(bf16)
    return high, middle, low


def key_bias(rows, length):
    key = lax.broadcasted_iota(jnp.int32, (rows, LANES), 0)
    return jnp.where(key < length, 0.0, DEAD).astype(bf16)


def attention_forward(qkv, mixed, stats, logs, length, width):
    rows = qkv.shape[0]
    lane = lax.broadcasted_iota(jnp.int32, (rows, LANES), 1)
    dead = key_bias(rows, length)
    zero = jnp.zeros((rows, LANES), bf16)
    one = jnp.ones((rows, LANES), bf16)

    def turn_of(turn, carry):
        def columns(part, head):
            at = part * width + (turn * FORWARD_PAIRS + head // 2) * LANES
            return pl.ds(pl.multiple_of(at, LANES), LANES)

        def marked(part, head, mark):
            own = (lane < HEAD) if head % 2 == 0 else (lane >= HEAD)
            mark = jnp.where(lane == HEAD - HEAD * (head % 2), mark, zero)
            return jnp.where(own, qkv[:, columns(part, head)], mark)

        def scores_of(head):
            return mm(marked(1, head, dead), marked(0, head, one), NT)

        heads = 2 * FORWARD_PAIRS
        ahead = [scores_of(0), scores_of(1)]
        outs = []
        for head in range(heads):
            if head + 2 < heads:
                ahead.append(scores_of(head + 2))
            scores = ahead[head]
            ahead[head] = None
            highest = jnp.max(scores, axis=0, keepdims=True)
            weights = jnp.exp(scores - highest).astype(bf16)
            product = mm(marked(2, head, one).T, weights)
            odd = head % 2
            total = product[HEAD - HEAD * odd : HEAD - HEAD * odd + 1]
            outs.append(product[HEAD * odd : HEAD * odd + HEAD] * (1.0 / total))
            logs[pl.ds(turn * heads + head, 1), :] = highest + jnp.log(total)
            if odd:
                mixed[:, columns(0, head)] = jnp.concatenate(outs, 0).T.astype(bf16)
                outs = []
        return carry

    turns = width // (FORWARD_PAIRS * LANES)
    if turns == 1:
        turn_of(0, 0)
    else:
        lax.fori_loop(0, turns, turn_of, 0)
    stats[:, :STAT_COLUMNS] = logs[...].T


def forward_block(weights, vec, need, length, saved, logs, unit1, unit2, result, send, done):
    w_qkv, w_out, w_in, w_back = weights
    x, qkv, mixed, stats, slope, active, normed = saved
    rows, width = x.shape
    half_rows = rows // 2
    scale = HEAD ** -0.5
    need("query")
    qkv[:, :width] = ((mm(x[...], w_qkv[:, :width]) + vec["bias_query"][...]) * scale).astype(bf16)
    need("key")
    qkv[:, width : 2 * width] = mm(x[...], w_qkv[:, width : 2 * width]).astype(bf16)
    qkv[:, 2 * width :] = (mm(x[...], w_qkv[:, 2 * width :]) + vec["bias_value"][...]).astype(bf16)
    attention_forward(qkv, mixed, stats, logs, length, width)
    lane = lax.broadcasted_iota(jnp.int32, (half_rows, LANES), 1)
    need("out")

    def after_attention(block, carry):
        rs = rows_at(block, half_rows)
        summed = x[rs, :].astype(f32) + mm(mixed[rs, :], w_out[...]) + vec["bias_out"][...]
        unit, factor = norm_rows(summed)
        unit1[rs, :] = unit
        normed[rs, :] = (unit * vec["gain_attn"][...] + vec["shift_attn"][...]).astype(bf16)
        stats[rs, :] = jnp.where(lane == FACTOR_ATTN, factor, stats[rs, :])
        return carry

    lax.fori_loop(0, 2, after_attention, 0)
    done("attn")
    need("in")
    need("back")

    def ffn(block, carry):
        rs = rows_at(block, half_rows)

        def hidden(j, carry):
            cs = rows_at(j, width)
            inner = mm(normed[rs, :], w_in[:, cs]) + vec["bias_in"][:, cs]
            share = 0.5 * (1.0 + lax.erf(inner * 0.7071067811865476))
            active[rs, cs] = (inner * share).astype(bf16)
            slope[rs, cs] = (
                share + inner * jnp.exp(-0.5 * inner * inner) * 0.3989422804014327
            ).astype(bf16)
            return carry

        lax.fori_loop(0, w_in.shape[1] // width, hidden, 0)
        summed = normed[rs, :].astype(f32) + mm(active[rs, :], w_back[...]) + vec["bias_back"][...]
        unit, factor = norm_rows(summed)
        unit2[rs, :] = unit
        result[rs, :] = (unit * vec["gain_ffn"][...] + vec["shift_ffn"][...]).astype(bf16)
        stats[rs, :] = jnp.where(lane == FACTOR_FFN, factor, stats[rs, :])
        send(block)
        return carry

    lax.fori_loop(0, 2, ffn, 0)
    done("ffn")


def attention_backward(qkv, gmix, mixed, stats, length, width, sums, between):
    rows = qkv.shape[0]
    lane = lax.broadcasted_iota(jnp.int32, (rows, LANES), 1)
    dead = key_bias(rows, length)
    zero = jnp.zeros((rows, LANES), bf16)
    one = jnp.ones((rows, LANES), bf16)

    def turn_of(turn, carry):
        heads = 2 * TURN_PAIRS

        def columns(part, head):
            at = part * width + (turn * TURN_PAIRS + head // 2) * LANES
            return pl.ds(pl.multiple_of(at, LANES), LANES)

        def log_total(head):
            if isinstance(turn, int):
                return stats[:, turn * heads + head : turn * heads + head + 1]
            logs = jnp.where(lane == turn * heads + head, stats[...], 0.0)
            return jnp.sum(logs, axis=-1, keepdims=True)

        def operands(head):
            q2, k2, v2 = [qkv[:, columns(part, head)] for part in range(3)]
            g2, mixed2 = gmix[:, columns(0, head)], mixed[:, columns(0, head)]
            own = (lane < HEAD) if head % 2 == 0 else (lane >= HEAD)
            at = HEAD - HEAD * (head % 2)
            terms = jnp.where(own, g2.astype(f32) * mixed2.astype(f32), 0.0)
            d0, d1, d2 = split_three(-jnp.sum(terms, axis=-1, keepdims=True))
            l0, l1, l2 = split_three(-log_total(head))
            m0, m1, m2, m3 = [lane == at + t for t in range(4)]
            m012 = m0 | m1 | m2
            qa = jnp.where(
                own,
                q2,
                jnp.where(m0, l0, jnp.where(m1, l1, jnp.where(m2, l2, jnp.where(m3, one, zero)))),
            )
            ga = jnp.where(own, g2, jnp.where(m0, d0, jnp.where(m1, d1, jnp.where(m2, d2, zero))))
            ka = jnp.where(own, k2, jnp.where(m012, one, jnp.where(m3, dead, zero)))
            va = jnp.where(own, v2, jnp.where(m012, one, zero))
            first = HEAD * (head % 2)
            return q2, g2, k2.T[first : first + HEAD], mm(ka, qa, NT), mm(va, ga, NT)

        ahead = operands(0)
        grads = []
        for head in range(heads):
            q2, g2, k2_t, scores, grad_probs = ahead
            if head + 1 < heads:
                ahead = operands(head + 1)
            probs = jnp.exp(scores)
            grad_scores = (probs * grad_probs).astype(bf16)
            grads.append((mm(k2_t, grad_scores), mm(grad_scores, q2), mm(probs.astype(bf16), g2)))
            if head % 2:
                even, odd = grads
                grads = []
                grad_q = jnp.concatenate([even[0], odd[0]], 0).T * (HEAD ** -0.5)
                grad_k = jnp.where(lane < HEAD, even[1], odd[1])
                grad_v = jnp.where(lane < HEAD, even[2], odd[2])
                for part, grad in enumerate((grad_q, grad_k, grad_v)):
                    qkv[:, columns(part, head)] = grad.astype(bf16)
                cols = columns(0, head)
                sums["bias_query"][:, cols] += column_sum(grad_q)
                sums["bias_value"][:, cols] += column_sum(grad_v)
                between(turn * TURN_PAIRS + head // 2)
        return carry

    turns = width // (TURN_PAIRS * LANES)
    if turns == 1:
        turn_of(0, 0)
    else:
        lax.fori_loop(0, turns, turn_of, 0)


def backward_block(grad_of, unit_of, weights, vec, need, length, saved, work, sums, give, hook):
    w_qkv, w_out, w_in, w_back = weights
    qkv, mixed, stats, slope = saved
    unit, gouter, gatt, gmix, gsum = work
    rows, width = gsum.shape
    half_rows = rows // 2
    need("unit_ffn")

    def first(block, carry):
        rs = rows_at(block, half_rows)
        grad, unit_rows = grad_of(block), unit_of(block)
        factor = stats[rs, FACTOR_FFN : FACTOR_FFN + 1]
        sums["gain_ffn"][...] += column_sum(grad * unit_rows)
        sums["shift_ffn"][...] += column_sum(grad)
        grad_sum = norm_back(grad * vec["gain_ffn"][...], unit_rows, factor)
        gsum[rs, :] = grad_sum
        gouter[rs, :] = grad_sum.astype(bf16)
        sums["bias_back"][...] += column_sum(grad_sum)
        return carry

    lax.fori_loop(0, 2, first, 0)
    hook("first", 0)
    need("hidden")

    def hidden(j, carry):
        cs = rows_at(j, width)
        grad_inner = mm(gouter[...], w_back[cs, :], NT) * slope[:, cs].astype(f32)
        sums["bias_in"](j)[...] += column_sum(grad_inner)
        slope[:, cs] = grad_inner.astype(bf16)
        hook("hidden", j)
        return carry

    lax.fori_loop(0, w_in.shape[1] // width, hidden, 0)
    hook("hidden_end", 0)
    need("middle")

    def middle(block, carry):
        rs = rows_at(block, half_rows)
        grad = gsum[rs, :] + mm(slope[rs, :], w_in[...], NT)
        unit_rows = unit[rs, :]
        factor = stats[rs, FACTOR_ATTN : FACTOR_ATTN + 1]
        sums["gain_attn"][...] += column_sum(grad * unit_rows)
        sums["shift_attn"][...] += column_sum(grad)
        grad_sum = norm_back(grad * vec["gain_attn"][...], unit_rows, factor)
        gsum[rs, :] = grad_sum
        rounded = grad_sum.astype(bf16)
        gatt[rs, :] = rounded
        sums["bias_out"][...] += column_sum(grad_sum)
        gmix[rs, :] = mm(rounded, w_out[...], NT).astype(bf16)
        hook("middle", block)
        return carry

    lax.fori_loop(0, 2, middle, 0)
    hook("middle_end", 0)
    need("attention")
    attention_backward(
        qkv, gmix, mixed, stats, length, width, sums, lambda h: hook("attention", h)
    )
    hook("attention_end", 0)
    need("last")

    def last(block, carry):
        rs = rows_at(block, half_rows)
        give(block, gsum[rs, :] + mm(qkv[rs, :], w_qkv[...], NT))
        hook("last", block)
        return carry

    lax.fori_loop(0, 2, last, 0)


def layer_kernel(chips, *refs):
    (x_in, cotangent, w_qkv, w_out, w_in, w_back), refs = refs[:6], refs[6:]
    vec, refs = dict(zip(FORWARD_VECTORS, refs)), refs[len(FORWARD_VECTORS) :]
    lengths, refs = refs[0], refs[1:]
    acts_out, grad_out, blocks_out, sums_out, units_out, refs = *refs[:5], refs[5:]
    weights, refs = refs[:4], refs[4:]
    mixed_x, attended_qkv, stats, slope, active, normed, refs = *refs[:6], refs[6:]
    gouter, gmix, gsend, gsum, unit, totals, total_slots, refs = *refs[:7], refs[7:]
    logs, acc_first, slots, refs = *refs[:3], refs[3:]
    weight_sem, x_sem, g_sem, unit_sem, acts_sem, forth_send, forth_recv, refs = *refs[:7], refs[7:]
    back_send, back_recv, grad_sem, sib_send, sib_recv, sib_free, refs = *refs[:6], refs[6:]
    ring_send, ring_recv, share_send, share_recv, sum_send, sum_recv, refs = *refs[:6], refs[6:]
    out_sem, sum_out_sem = refs
    rank = lax.axis_index("section")
    me = lax.axis_index("dp")
    peer = (1 - rank, me)
    rows, width = gsum.shape
    half_rows = rows // 2
    mixed, x_kept = [mixed_x.at[:, pl.ds(k * width, width)] for k in range(2)]
    gatt = attended_qkv.at[:, pl.ds(0, width)]
    qkv = attended_qkv.at[:, pl.ds(width, 3 * width)]

    core = lax.rem(me, 2)
    chip = lax.div(me, 2)
    ring_half = chips // 2
    place = jnp.where(lax.rem(chip, 2) == 0, lax.div(chip, 2), chips - 1 - lax.div(chip, 2))
    rounds, _, subs = ring_recv.shape[:3]
    piece = -(-width // (16 * subs * chips)) * 16 * subs
    part = piece // subs
    steps = chips - 1
    bits = total_slots.shape[0]

    def device_at(position):
        position = lax.rem(position + chips, chips)
        spot = jnp.where(position < ring_half, 2 * position, 2 * (chips - 1 - position) + 1)
        return (rank, 2 * spot + core)

    sibling = (rank, me + 1 - 2 * core)
    def way_to(way):
        return device_at(place + 1 - 2 * way)

    def across(bit):
        size = 1 << bit
        return (rank, me + size - 2 * size * lax.rem(lax.div(me, size), 2))

    def half_at(i, block):
        return pl.ds(pl.multiple_of(i * rows + block * half_rows, half_rows), half_rows)

    query = pl.ds(0, width)
    key_value = pl.ds(width, 2 * width)
    loads = dict(
        query=(w_qkv.at[0, :, query], weights[0].at[:, query]),
        key=(w_qkv.at[0, :, key_value], weights[0].at[:, key_value]),
        out=(w_out.at[0], weights[1]),
        back=(w_back.at[0], weights[3]),
    )
    loads["in"] = (w_in.at[0], weights[2])
    order = ("query", "key", "out", "in", "back")
    loads = {
        name: pltpu.make_async_copy(*loads[name], weight_sem.at[k]) for k, name in enumerate(order)
    }

    def x_load(i):
        rs = rows_at(i, rows)
        return pltpu.make_async_copy(x_in.at[rs], x_kept.at[rs], x_sem.at[i])

    def g_load():
        return pltpu.make_async_copy(cotangent, gouter, g_sem)

    @pl.when(rank == 0)
    def _():
        x_load(0).start()

    loads["query"].start()
    loads["key"].start()
    barrier = pltpu.get_barrier_semaphore()
    partners = [peer, sibling, way_to(0), way_to(1)] + [across(bit) for bit in range(1, bits)]
    for partner in partners:
        pl.semaphore_signal(barrier, inc=1, device_id=partner, device_id_type=MESH)
    totals[...] = jnp.zeros_like(totals)
    sums = {name: totals.at[pl.ds(k, 1)] for k, name in enumerate(SUM_ROWS)}
    sums["bias_in"] = lambda j: totals.at[pl.ds(len(SUM_ROWS) + j, 1)]
    pl.semaphore_wait(barrier, len(partners))

    def forth(i, block):
        rs = half_at(i, block)
        return pltpu.make_async_remote_copy(
            src_ref=gatt.at[rs],
            dst_ref=x_kept.at[rs],
            send_sem=forth_send.at[i, block],
            recv_sem=forth_recv.at[i, block],
            device_id=peer,
            device_id_type=MESH,
        )

    def acts_copy(i):
        rs = rows_at(i, rows)
        return pltpu.make_async_copy(gatt.at[rs], acts_out.at[rs], acts_sem.at[i])

    def spill(k):
        return pltpu.make_async_copy((unit, gsum)[k], units_out.at[k], unit_sem.at[k])

    def unspill(k):
        return pltpu.make_async_copy(units_out.at[k], unit, unit_sem.at[k])

    def forward_batch(i, carry):
        mine = rows_at(i, rows)

        @pl.when(rank == 0)
        def _():
            x_load(i).wait()

        @pl.when(rank == 1)
        def _():
            forth(i, 0).wait_recv()
            forth(i, 1).wait_recv()

        def need(what):
            @pl.when(i == 0)
            def _():
                loads[what].wait()
                if what == "key":
                    loads["out"].start()
                    loads["in"].start()
                    loads["back"].start()
                if what == "out":

                    @pl.when(rank == 0)
                    def _():
                        x_load(1).start()

                    @pl.when(rank == 1)
                    def _():
                        g_load().start()

            if what in ("out", "back"):

                @pl.when(i > 0)
                def _():
                    spill(0 if what == "out" else 1).wait()

        def done(what):
            @pl.when(i < MB - 1)
            def _():
                spill(0 if what == "attn" else 1).start()

            if what == "ffn":
                acts_copy(i).start()

        def send(block):
            @pl.when(rank == 0)
            def _():
                forth(i, block).start()

        forward_block(
            weights,
            vec,
            need,
            lengths[i],
            [ref.at[mine] for ref in (x_kept, qkv, mixed, stats, slope, active, normed)],
            logs,
            unit,
            gsum,
            gatt.at[mine],
            send,
            done,
        )
        return carry

    lax.fori_loop(0, MB, forward_batch, 0)

    def acc(r, way, rs=None):
        rs = pl.ds(0, width) if rs is None else rs
        if r == 0:
            return acc_first.at[way, rs]
        return weights[3].at[pl.ds(pl.multiple_of((2 * r - 2 + way) * width + rs.start, 16), rs.size)]

    def sibling_term(r, way):
        if r == 0:
            return slots.at[1, way]
        return active.at[pl.ds(0, width), rows_at(way, width)]

    tiles = 2
    tile_rows = width // tiles
    first_tile = jnp.minimum(lax.div(place * piece, tile_rows), tiles - 1)

    def to_sibling(r, way, tile):
        here = rows_at(tile, tile_rows)
        return pltpu.make_async_remote_copy(
            src_ref=acc(r, way, here),
            dst_ref=sibling_term(r, way).at[here],
            send_sem=sib_send.at[way, tile],
            recv_sem=sib_recv.at[way, tile],
            device_id=sibling,
            device_id_type=MESH,
        )

    def term(r, owner, way, tile):
        j = 2 * owner + way
        left, at, right = (
            (active, j * width, gouter),
            (normed, 0, slope.at[:, rows_at(j, width)]),
            (mixed_x, jnp.minimum(j, 1) * width, attended_qkv.at[:, rows_at(j, width)]),
        )[r]
        cs = pl.ds(pl.multiple_of(at + tile * tile_rows, LANES), tile_rows)
        return mm(left[:, cs], right[...], TN)

    def compute(r, between):
        if r > 0:
            pl.semaphore_wait(sib_free, 1)

        def one_tile(step, carry):
            tile = lax.rem(first_tile + step, tiles)
            here = rows_at(tile, tile_rows)

            def for_sibling(way, carry):
                acc(r, way, here)[...] = term(r, 1 - core, way, tile).astype(bf16)
                to_sibling(r, way, tile).start()
                return carry

            def for_me(way, carry):
                value = term(r, core, way, tile)
                to_sibling(r, way, tile).wait()
                other = sibling_term(r, way).at[here]
                acc(r, way, here)[...] = (value + other[...].astype(f32)).astype(bf16)
                return carry

            lax.fori_loop(0, 2, for_sibling, 0)
            lax.fori_loop(0, 2, for_me, 0)

            @pl.when(step == 0)
            def _():
                between()

            return carry

        lax.fori_loop(0, tiles, one_tile, 0)
        if r < rounds - 1:
            pl.semaphore_signal(sib_free, inc=1, device_id=sibling, device_id_type=MESH)

    def rows_of(way, sub, t):
        sign = 1 - 2 * way
        index = lax.rem(place - sign * t + 2 * chips, chips)
        return pl.ds(pl.multiple_of(index * piece + sub * part, 16), part)

    def ring(r, way, sub, t, target):
        return pltpu.make_async_remote_copy(
            src_ref=acc(r, way, rows_of(way, sub, t)),
            dst_ref=target,
            send_sem=ring_send.at[r, way, sub, lax.rem(t, 2)],
            recv_sem=ring_recv.at[r, way, sub, t],
            device_id=way_to(way),
            device_id_type=MESH,
        )

    def adding(r, way, sub, t):
        return ring(r, way, sub, t, slots.at[r, way, rows_of(way, sub, t)])

    def handing(r, way, sub, t):
        return ring(r, way, sub, t, acc(r, way, rows_of(way, sub, t)))

    def share(r, way, rs):
        return pltpu.make_async_remote_copy(
            src_ref=acc(r, way, rs),
            dst_ref=blocks_out.at[4 * r + 2 * core + way, rs],
            send_sem=share_send.at[r, way],
            recv_sem=share_recv.at[r, way],
            device_id=sibling,
            device_id_type=MESH,
        )

    def place_out(r, way, rs):
        block = blocks_out.at[4 * r + 2 * core + way, rs]
        return pltpu.make_async_copy(acc(r, way, rs), block, out_sem.at[r, way])

    def when(condition, way, t, body):
        if chips * piece > width:
            condition = condition & (rows_of(way, 0, t).start < width)
        if condition is True:
            body()
        elif condition is not False:
            pl.when(condition)(body)

    def chain(r, way, sub, t):
        def sent():
            adding(r, way, sub, t - 2).wait_send()

        def added():
            adding(r, way, sub, t - 1).wait_recv()
            rs = rows_of(way, sub, t)
            acc(r, way, rs)[...] = (
                acc(r, way, rs)[...].astype(f32) + slots[r, way, rs].astype(f32)
            ).astype(bf16)

        def kept():
            handing(r, way, sub, t - 1).wait_recv()

        def whole():
            share(r, way, rows_of(way, sub, t)).start()
            place_out(r, way, rows_of(way, sub, t)).start()

        when((t >= 2) & (t <= 2 * steps + 1), way, t - 2, sent)
        when((t >= 1) & (t <= steps), way, t, added)
        when((t >= 0) & (t < steps), way, t, lambda: adding(r, way, sub, t).start())
        when((t > steps) & (t <= 2 * steps), way, t, kept)
        when((t >= steps) & (t < 2 * steps), way, t, lambda: handing(r, way, sub, t).start())
        when((t >= steps) & (t <= 2 * steps), way, t, whole)

    def slot(tick, offsets):
        for r, offset in enumerate(offsets):

            def one_chain(k, carry):
                chain(r, lax.rem(k, 2), lax.div(k, 2), tick - offset)
                return carry

            lax.fori_loop(0, 2 * subs, one_chain, 0)

    def back(i, block):
        return pltpu.make_async_remote_copy(
            src_ref=gsend.at[rows_at(block, half_rows)],
            dst_ref=gouter.at[half_at(i, block)],
            send_sem=back_send.at[block],
            recv_sem=back_recv.at[i, block],
            device_id=peer,
            device_id_type=MESH,
        )

    def grad_copy(i, block):
        source = gsum.at[rows_at(block, half_rows)]
        return pltpu.make_async_copy(source, grad_out.at[half_at(i, block)], grad_sem.at[block])

    early = (0, 4, 11)
    early_ticks = 15

    def backward_batch(turn, rank, hooked):
        i = MB - 1 - turn
        mine = rows_at(i, rows)

        def need(what):
            if what == "unit_ffn":

                @only_if((turn == 0) & (rank == 1))
                def _():
                    g_load().wait()

                @only_if(turn > 0)
                def _():
                    unspill(1).wait()
                    for block in (0, 1):
                        grad_copy(MB - 1, block).wait()

            if what == "hidden":

                @only_if(turn > 0)
                def _():
                    unspill(0).start()

            if what == "middle":

                @only_if(turn == 0)
                def _():
                    for k in range(MB):
                        acts_copy(k).wait()

                        @only_if(rank == 0)
                        def _():
                            for block in (0, 1):
                                forth(k, block).wait_send()

                @only_if(turn > 0)
                def _():
                    unspill(0).wait()

            if what == "attention":

                @only_if(turn == 0)
                def _():
                    unspill(1).start()

        def hook(what, k):
            if what == "attention" and k % 2 == 0:
                return

            @only_if((turn == MB - 1) & (rank == 0))
            def _():
                ring_part(what, k)

        def ring_part(what, k):

            def at(condition, tick, rounds_now):
                @only_if(condition)
                def _():
                    slot(tick, early[:rounds_now])

            if what == "first":
                compute(0, lambda: slot(0, early[:1]))
                slot(1, early[:1])
            if what == "hidden":
                at(lax.rem(k, 2) == 1, 2 + lax.div(k, 2), 1)
            if what == "hidden_end":
                compute(1, lambda: slot(4, early[:2]))
                slot(5, early[:2])
            if what == "middle":
                slot(6 + k, early[:2])
            if what == "attention" and k % 2 == 1:
                slot(8 + k // 2, early[:2])
            if what == "attention_end":
                compute(2, lambda: slot(11, early))
                slot(12, early)
                slot(13, early)
            if what == "last":
                at(k == 1, 14, 3)

        def grad_of(block):
            @only_if(rank == 0)
            def _():
                back(i, block).wait_recv()

            return gouter[half_at(i, block), :].astype(f32)

        def unit_of(block):
            rs = rows_at(block, half_rows)
            if isinstance(turn, int):
                return (gsum if turn == 0 else unit)[rs, :]
            return jnp.where(turn == 0, gsum[rs, :], unit[rs, :])

        def give(block, value):
            @only_if((turn > 0) & (rank == 1))
            def _():
                back(MB - 1, block).wait_send()

            rs = rows_at(block, half_rows)
            rounded = value.astype(bf16)
            gsend[rs, :] = rounded
            if hooked:
                gsum[rs, :] = value
            else:
                gsum[rs, :] = jnp.where(rank == 1, rounded.astype(f32), value)
            grad_copy(i, block).start()

            @only_if(rank == 1)
            def _():
                back(i, block).start()

        backward_block(
            grad_of,
            unit_of,
            weights,
            vec,
            need,
            lengths[i],
            [ref.at[mine] for ref in (qkv, mixed, stats, slope)],
            (unit, gouter.at[mine], gatt.at[mine], gmix, gsum),
            sums,
            give,
            hook,
        )

    def plain(turn, carry):
        backward_batch(turn, rank, False)
        return carry

    lax.fori_loop(0, MB, plain, 0)


    def sum_step(bit):
        return pltpu.make_async_remote_copy(
            src_ref=totals,
            dst_ref=total_slots.at[bit],
            send_sem=sum_send.at[bit],
            recv_sem=sum_recv.at[bit],
            device_id=across(bit),
            device_id_type=MESH,
        )

    late = (0, 2, 4)
    late_ticks = 6

    @pl.when(rank == 1)
    def _():
        for r in range(rounds):
            compute(r, lambda: slot(2 * r, late[: r + 1]))
            slot(2 * r + 1, late[: r + 1])

    start = jnp.where(rank == 0, early_ticks, late_ticks)
    offsets = [jnp.where(rank == 0, early[r], late[r]) for r in range(rounds)]

    def rest(tick, carry):
        slot(tick, offsets)
        for bit in range(bits + 1):

            @pl.when(tick - start == 2 + bit)
            def _():
                if bit > 0:
                    sum_step(bit - 1).wait()
                    totals[...] += total_slots[bit - 1]
                if bit < bits:
                    sum_step(bit).start()

        return carry

    lax.fori_loop(start, offsets[-1] + 2 * steps + 2, rest, 0)
    sum_copy = pltpu.make_async_copy(totals, sums_out, sum_out_sem)
    sum_copy.start()
    for block in (0, 1):
        grad_copy(0, block).wait()

        @pl.when(rank == 1)
        def _():
            back(0, block).wait_send()

    everything = pl.ds(0, width)
    for r in range(rounds):
        for way in (0, 1):
            share(r, way, everything).wait_recv()
            share(r, way, everything).wait_send()
            place_out(r, way, everything).wait()
    sum_copy.wait()


def finish_kernel(acts, grads, blocks, sums, *refs):
    acts_out, grads_out, refs = refs[0], refs[1], refs[2:]
    outs, vectors, refs = refs[:4], refs[4 : 4 + len(SUM_ROWS) + 1], refs[5 + len(SUM_ROWS) :]
    taken, wide, acts_kept, grads_kept, in_sem, out_sem, copy_sem = refs
    depth, width = taken.shape[0], sums.shape[1]
    ways = ((acts, acts_kept, acts_out), (grads, grads_kept, grads_out))
    copies_in = [
        pltpu.make_async_copy(source, kept, copy_sem.at[k])
        for k, (source, kept, _) in enumerate(ways)
    ]
    copies_out = [
        pltpu.make_async_copy(kept, out.at[0], copy_sem.at[k])
        for k, (_, kept, out) in enumerate(ways)
    ]

    def target(k):
        if k < 4:
            return outs[0].at[0, pl.ds(k * width, width)]
        if k < 8:
            return outs[1].at[0, :, pl.ds((k - 4) * width, width)]
        if k < 9:
            return outs[2].at[0]
        return outs[3].at[0, :, pl.ds((k - 9) * width, width)]

    def load(k):
        return pltpu.make_async_copy(blocks.at[k], taken.at[k % depth], in_sem.at[k % depth])

    def store(k):
        return pltpu.make_async_copy(wide.at[k % depth], target(k), out_sem.at[k % depth])

    count = blocks.shape[0]
    for k in range(depth):
        load(k).start()
    for copy in copies_in:
        copy.start()
    for k, out in enumerate(vectors[:-1]):
        out[...] = sums[k : k + 1, :]
    for j in range(vectors[-1].shape[1] // width):
        row = len(SUM_ROWS) + j
        vectors[-1][:, j * width : (j + 1) * width] = sums[row : row + 1, :]
    for k in range(count):
        load(k).wait()
        if k >= depth:
            store(k - depth).wait()
        wide[k % depth] = taken[k % depth].astype(f32)
        store(k).start()
        if k + depth < count:
            load(k + depth).start()
        elif k + depth == count:
            for copy_in, copy_out in zip(copies_in, copies_out):
                copy_in.wait()
                copy_out.start()
    for k in range(count - depth, count):
        store(k).wait()
    for copy in copies_out:
        copy.wait()


def per_device(chips, *args):
    x_input = args[0]
    names = (
        "w_qkv", "bias_query", "bias_value", "w_out", "bias_out", "gain_attn", "shift_attn",
        "w_in", "bias_in", "w_back", "bias_back", "gain_ffn", "shift_ffn",
    )
    given = dict(zip(names, args[1:14]))
    lengths, cotangent = args[14:]
    row_count, width = x_input.shape
    rows = row_count // MB
    hidden = given["w_in"].shape[2]
    weights = [given[name] for name in ("w_qkv", "w_out", "w_in", "w_back")]
    anywhere = pl.BlockSpec(memory_space=pl.ANY)
    vmem = pl.BlockSpec(memory_space=pltpu.VMEM)
    smem = pl.BlockSpec(memory_space=pltpu.SMEM)
    dma = pltpu.SemaphoreType.DMA
    shape = jax.ShapeDtypeStruct
    weight_scratch = [pltpu.VMEM(w.shape[1:], bf16) for w in weights]
    kept = [
        (2 * width, bf16),
        (4 * width, bf16),
        (LANES, f32),
        (hidden, bf16),
        (hidden, bf16),
        (width, bf16),
    ]
    rounds = (3 * width + width + 2 * hidden) // (4 * width)
    subs = 3 if width % (48 * chips) == 0 else 1
    steps = chips - 1
    bits = (2 * chips).bit_length() - 1
    square = (width, width)

    def whole_rows(columns):
        return [pltpu.VMEM((row_count, n), kind) for n, kind in columns]

    acts, input_grads, blocks, totals, _ = pl.pallas_call(
        functools.partial(layer_kernel, chips),
        out_shape=[
            shape((row_count, width), bf16),
            shape((row_count, width), f32),
            shape((4 * rounds, *square), bf16),
            shape((SUM_COUNT, width), f32),
            shape((2, rows, width), f32),
        ],
        in_specs=[anywhere] * 6 + [vmem] * len(FORWARD_VECTORS) + [smem],
        out_specs=[anywhere] * 5,
        scratch_shapes=weight_scratch
        + whole_rows(kept)
        + whole_rows([(width, bf16)])
        + [
            pltpu.VMEM((rows, width), bf16),
            pltpu.VMEM((rows, width), bf16),
            pltpu.VMEM((rows, width), f32),
            pltpu.VMEM((rows, width), f32),
            pltpu.VMEM((SUM_COUNT, width), f32),
            pltpu.VMEM((bits, SUM_COUNT, width), f32),
            pltpu.VMEM((STAT_COLUMNS, rows), f32),
            pltpu.VMEM((2, *square), bf16),
            pltpu.VMEM((rounds, 2, *square), bf16),
            dma((5,)),
            dma((MB,)),
            dma,
            dma((2,)),
            dma((MB,)),
            dma((MB, 2)),
            dma((MB, 2)),
            dma((2,)),
            dma((MB, 2)),
            dma((2,)),
            dma((2, 2)),
            dma((2, 2)),
            pltpu.SemaphoreType.REGULAR,
            dma((rounds, 2, subs, 2)),
            dma((rounds, 2, subs, 2 * steps)),
            dma((rounds, 2)),
            dma((rounds, 2)),
            dma((bits,)),
            dma((bits,)),
            dma((rounds, 2)),
            dma,
        ],
        compiler_params=pltpu.CompilerParams(
            collective_id=0, has_side_effects=True, vmem_limit_bytes=VMEM_LIMIT
        ),
        name="layer",
    )(x_input, cotangent, *weights, *[given[name] for name in FORWARD_VECTORS], lengths)
    vector_names = SUM_ROWS + ("bias_in",)
    depth = 4
    acts, input_grads, *whole = pl.pallas_call(
        finish_kernel,
        out_shape=[
            shape((1, row_count, width), bf16),
            shape((1, row_count, width), f32),
            shape((1, hidden, width), f32),
            shape((1, width, hidden), f32),
            shape((1, width, width), f32),
            shape((1, width, 3 * width), f32),
        ]
        + [shape(given[name].shape, f32) for name in vector_names],
        in_specs=[anywhere] * 3 + [vmem],
        out_specs=[anywhere] * 6 + [vmem] * len(vector_names),
        scratch_shapes=[
            pltpu.VMEM((depth, *square), bf16),
            pltpu.VMEM((depth, *square), f32),
            pltpu.VMEM((row_count, width), bf16),
            pltpu.VMEM((row_count, width), f32),
            dma((depth,)),
            dma((depth,)),
            dma((2,)),
        ],
        compiler_params=pltpu.CompilerParams(vmem_limit_bytes=VMEM_LIMIT),
        name="finish",
    )(acts, input_grads, blocks, totals)
    grads = dict(zip(("w_back", "w_in", "w_out", "w_qkv") + vector_names, whole))
    return (acts, input_grads, *[grads[name] for name in names])


def solution(mesh):
    return jax.shard_map(
        functools.partial(per_device, mesh.shape["dp"] // 2),
        mesh=mesh,
        in_specs=(
            P("dp", None),
            P("section", None, None),
            P("section", None),
            P("section", None),
            P("section", None, None),
            P("section", None),
            P("section", None),
            P("section", None),
            P("section", None, None),
            P("section", None),
            P("section", None, None),
            P("section", None),
            P("section", None),
            P("section", None),
            P("dp"),
            P("dp", None),
        ),
        out_specs=(
            P("section", "dp", None),
            P("section", "dp", None),
            P("section", None, None),
            P("section", None),
            P("section", None),
            P("section", None, None),
            P("section", None),
            P("section", None),
            P("section", None),
            P("section", None, None),
            P("section", None),
            P("section", None, None),
            P("section", None),
            P("section", None),
            P("section", None),
        ),
        check_vma=False,
    )
```
